256 devices in a mesh: dp: 64 (over y, z, core), mp: 4 (over x).
Axes of the slice: x: 4, y: 4, z: 8, core: 2. Of those that a mesh axis runs over, the one named last changes fastest.
Arguments:
- queries: bfloat16 [8192, 4096], P('dp', 'mp'), may hold values from -6 to 6
- cotangent: bfloat16 [8192, 4096], P('dp', 'mp'), may hold values from -6 to 6
- neighbours: bfloat16 [128, 2, 128, 896], P('dp', None, 'mp'), may hold values from -16 to 16
- present: int32 [128, 2], P('dp'), may hold values 0 or 1
- key_weight: bfloat16 [896, 4096], P(None, 'mp'), may hold values from -0.1875 to 0.1875
- value_weight: bfloat16 [896, 4096], P(None, 'mp'), may hold values from -0.1875 to 0.1875
Outputs:
- attended: bfloat16 [8192, 4096], P('dp', 'mp')
- query_grad: bfloat16 [8192, 4096], P('dp', 'mp')
- neighbour_grad: float32 [128, 2, 128, 896], P('dp', None, 'mp')
- key_weight_grad: float32 [896, 4096], P('dp', 'mp')
- value_weight_grad: float32 [896, 4096], P('dp', 'mp')
The draws below stay inside these ranges and needn't reach their ends.
All inputs are finite; a program needn't handle non-finite values. No bound on the sum of `present` on one device may be relied on, other than what follows from the above.
Results may differ from the reference program's by a relative error of at most 0.014.
Values may be sent and summed in bfloat16 or wider, within the bound.
No kernel may reach another device: no remote copies, remote signals or barrier semaphores. Data moves between devices by JAX's collectives and lax.ppermute only.
A program may use at most 128 MiB of HBM per device.

```python
import jax
import jax.numpy as jnp
from jax import lax

D_ENC = 896
HEADS = 32
HEAD = 128
STRETCH = 64
NEIGH = 2
PASS = 128
STRETCHES = 128
TOKENS = 8192
WIDTH = 4096


def set_ends(values, stream_key, low, high):
    shape = values.shape
    spot = [jax.random.randint(jax.random.fold_in(stream_key, axis), (), 0, shape[axis]) for axis in range(len(shape))]
    values = values.at[tuple(spot)].set(low)
    longest = shape.index(max(shape))
    spot[longest] = (spot[longest] + 1) % shape[longest]
    return values.at[tuple(spot)].set(high)


def strengthened(array, stream_key, source, target, shards_of, factor):
    owner, partner = [(jnp.arange(array.shape[position]) // (array.shape[position] // shards_of)).reshape([-1 if axis == position else 1 for axis in range(array.ndim)]) for position in (source, target)]
    chosen = jax.random.permutation(stream_key, shards_of)[partner]
    strong = (owner == chosen) | (owner == (partner + shards_of // 2) % shards_of)
    return jnp.where(strong, factor * array, array)


def block_scale(rng, shape, pieces, smallest, high):
    def one(axis_at, shards_of):
        draws = jax.random.uniform(jax.random.fold_in(jax.random.fold_in(rng, 6), axis_at), (shards_of,), jnp.float32, smallest / len(pieces), high / len(pieces))
        return jnp.repeat(jnp.exp(draws), shape[axis_at] // shards_of).reshape((-1,) + (1,) * (len(shape) - axis_at - 1))

    gain = one(*pieces[0])
    for cut in pieces[1:]:
        gain = gain * one(*cut)
    return gain


def normal_values(stream_key, dims, spread, limit, cuts=(), dtype=jnp.bfloat16):
    drawn = spread * jax.random.normal(stream_key, dims, jnp.float32)
    if cuts:
        drawn = drawn * block_scale(stream_key, dims, cuts, -0.22, 0.18)
    return jnp.clip(drawn, -limit, limit).astype(dtype)


def heavy_noise(stream_key, dims, scale, bound, cuts, heavy, dtype=jnp.bfloat16):
    array = scale * jax.random.normal(stream_key, dims, jnp.float32)
    if cuts:
        array = array * block_scale(stream_key, dims, cuts, -0.22, 0.18)
    return jnp.clip(strengthened(array, jax.random.fold_in(stream_key, 3), *heavy), -bound, bound).astype(dtype)


def setup_inputs(seed: int = 0) -> dict:
    streams_of = jax.random.split(jax.random.key(seed), 7)
    queries = normal_values(streams_of[0], (TOKENS, WIDTH), 1.0, 6.0, ((0, 64), (1, 4)))
    cotangent = normal_values(streams_of[1], (TOKENS, WIDTH), 1.0, 6.0, ((0, 64), (1, 4)))
    neighbours = heavy_noise(streams_of[2], (STRETCHES, NEIGH, PASS, D_ENC), 1.0, 16.0, ((0, 64), (2, 4)), (0, 3, 64, 4.0))
    present = set_ends((jax.random.randint(streams_of[3], (STRETCHES, NEIGH), 0, 4) < 3).astype(jnp.int32), jax.random.fold_in(streams_of[3], 1), 0, 1)
    key_weight = normal_values(streams_of[4], (D_ENC, WIDTH), D_ENC ** -0.5, 0.1875, ((1, 4),))
    value_weight = normal_values(streams_of[5], (D_ENC, WIDTH), D_ENC ** -0.5, 0.1875, ((1, 4),))
    return dict(queries=queries, cotangent=cotangent, neighbours=neighbours, present=present, key_weight=key_weight, value_weight=value_weight)


def reference(queries, cotangent, neighbours, present, key_weight, value_weight):
    score_scale = HEAD ** -0.5
    key_span = NEIGH * PASS
    query_blocks = queries.reshape(STRETCHES, STRETCH, HEADS, HEAD)
    grad_blocks = cotangent.reshape(STRETCHES, STRETCH, HEADS, HEAD)

    def one_stretch(grad_sums, inputs):
        query_block, grad_block, passages, flags = inputs
        flat_rows = passages.reshape(key_span, D_ENC)
        key_rows = jnp.dot(flat_rows, key_weight, preferred_element_type=jnp.float32).astype(jnp.bfloat16)
        value_rows = jnp.dot(flat_rows, value_weight, preferred_element_type=jnp.float32).astype(jnp.bfloat16)
        query_heads = query_block.astype(jnp.float32)
        key_heads = key_rows.reshape(key_span, HEADS, HEAD).astype(jnp.float32)
        value_heads = value_rows.reshape(key_span, HEADS, HEAD).astype(jnp.float32)
        scores = jnp.einsum("thd,rhd->htr", query_heads, key_heads) * score_scale
        live_keys = jnp.repeat(flags.astype(jnp.float32), PASS)
        raw_weights = jnp.exp(scores) * live_keys
        no_keys = (jnp.sum(flags) == 0).astype(jnp.float32)
        weights = raw_weights / (jnp.sum(raw_weights, axis=-1, keepdims=True) + no_keys)
        weights_low = lax.optimization_barrier(weights.astype(jnp.bfloat16)).astype(jnp.float32)
        attended = jnp.einsum("htr,rhd->thd", weights_low, value_heads).astype(jnp.bfloat16)
        grad_heads = grad_block.astype(jnp.float32)
        prob_grad = jnp.einsum("thd,rhd->htr", grad_heads, value_heads)
        row_delta = jnp.sum(weights * prob_grad, axis=-1, keepdims=True)
        score_grad = weights * (prob_grad - row_delta) * score_scale
        score_grad = lax.optimization_barrier(score_grad.astype(jnp.bfloat16)).astype(jnp.float32)
        value_grad = jnp.einsum("htr,thd->rhd", weights_low, grad_heads).astype(jnp.bfloat16)
        query_grad = jnp.einsum("htr,rhd->thd", score_grad, key_heads).astype(jnp.bfloat16)
        key_grad = jnp.einsum("htr,thd->rhd", score_grad, query_heads).astype(jnp.bfloat16)
        key_grad_rows = key_grad.reshape(key_span, WIDTH)
        value_grad_rows = value_grad.reshape(key_span, WIDTH)
        key_sum = grad_sums[0] + jnp.dot(flat_rows.T, key_grad_rows, preferred_element_type=jnp.float32)
        value_sum = grad_sums[1] + jnp.dot(flat_rows.T, value_grad_rows, preferred_element_type=jnp.float32)
        passage_grad = jnp.dot(key_grad_rows, key_weight.T, preferred_element_type=jnp.float32)
        passage_grad = passage_grad + jnp.dot(value_grad_rows, value_weight.T, preferred_element_type=jnp.float32)
        outputs = (attended.reshape(STRETCH, WIDTH), query_grad.reshape(STRETCH, WIDTH), passage_grad.reshape(NEIGH, PASS, D_ENC))
        return (key_sum, value_sum), outputs

    zeros = jnp.zeros((D_ENC, WIDTH), jnp.float32)
    sums, stacked = lax.scan(one_stretch, (zeros, zeros), (query_blocks, grad_blocks, neighbours, present))
    attended = stacked[0].reshape(TOKENS, WIDTH)
    query_grad = stacked[1].reshape(TOKENS, WIDTH)
    return attended, query_grad, stacked[2], sums[0], sums[1]
```

```python
import jax
import jax.numpy as jnp
from jax import lax
from jax.experimental import pallas as pl
from jax.experimental.pallas import tpu as pltpu
from jax.sharding import Mesh, PartitionSpec as P

HEAD = 128
BF = jnp.bfloat16
F32 = jnp.float32
NT = (((1,), (1,)), ((), ()))
TN = (((0,), (0,)), ((), ()))
VMEM_LIMIT = 48 * 1024 * 1024


def ring(size, step):
    return [(i, (i + step) % size) for i in range(size)]


def dot(a, b, dims=(((1,), (0,)), ((), ()))):
    return lax.dot_general(a, b, dims, preferred_element_type=F32)


def attend_body(
    stretches, span, group, steps,
    flags, rows, key_w, value_w, queries, cotangent,
    attended, query_grad, keep, send, passage, total,
):
    step = pl.program_id(0)
    core = flags[0]
    tokens = queries.shape[0] // stretches
    scale = HEAD ** (-0.5)
    keys = dot(rows[...], key_w[...]).astype(BF)
    values = dot(rows[...], value_w[...]).astype(BF)
    neigh = (lax.broadcasted_iota(jnp.int32, (1, span), 1) // group) % 2
    key_grads, value_grads = [], []
    for c in range(stretches):
        first, second = flags[1 + 2 * c], flags[2 + 2 * c]
        live = jnp.where(neigh == 0, first, second).astype(F32)
        empty = jnp.where(first + second == 0, 1.0, 0.0).astype(F32)
        r = slice(c * span, (c + 1) * span)
        t = slice(c * tokens, (c + 1) * tokens)
        kg_heads, vg_heads = [], []
        for h in range(queries.shape[1] // HEAD):
            w = slice(h * HEAD, (h + 1) * HEAD)
            q, g = queries[t, w], cotangent[t, w]
            k, v = keys[r, w], values[r, w]
            raw = jnp.exp(dot(q, k, NT) * scale) * live
            probs = raw / (jnp.sum(raw, axis=-1, keepdims=True) + empty)
            low = probs.astype(BF)
            attended[t, w] = dot(low, v).astype(BF)
            prob_grad = dot(g, v, NT)
            delta = jnp.sum(probs * prob_grad, axis=-1, keepdims=True)
            score_grad = (probs * (prob_grad - delta) * scale).astype(BF)
            query_grad[t, w] = dot(score_grad, k).astype(BF)
            vg_heads.append(dot(low, g, TN).astype(BF))
            kg_heads.append(dot(score_grad, q, TN).astype(BF))
        key_grads.append(jnp.concatenate(kg_heads, axis=1))
        value_grads.append(jnp.concatenate(vg_heads, axis=1))
    key_grad = jnp.concatenate(key_grads, axis=0)
    value_grad = jnp.concatenate(value_grads, axis=0)

    @pl.when(core == 0)
    def _():
        keep[...] = key_grad
        send[...] = value_grad

    @pl.when(core != 0)
    def _():
        keep[...] = value_grad
        send[...] = key_grad

    part = dot(key_grad, key_w[...], NT) + dot(value_grad, value_w[...], NT)

    @pl.when(step == 0)
    def _():
        total[...] = part

    @pl.when(step > 0)
    def _():
        total[...] += part

    @pl.when(step == steps - 1)
    def _():
        passage[...] = total[...].astype(BF)


def attend(flags, rows, key_w, value_w, queries, cotangent, stretches, group):
    row_count, enc = rows.shape
    tokens, width = queries.shape
    block = 2 * HEAD
    steps = width // block
    span = row_count // stretches

    def body(*refs):
        attend_body(stretches, span, group, steps, *refs)

    columns = lambda n: pl.BlockSpec((n, block), lambda i: (0, i))
    whole = pl.BlockSpec((row_count, enc), lambda i: (0, 0))
    return pl.pallas_call(
        body,
        grid=(steps,),
        in_specs=[
            pl.BlockSpec(memory_space=pltpu.SMEM),
            whole,
            columns(enc),
            columns(enc),
            columns(tokens),
            columns(tokens),
        ],
        out_specs=[
            columns(tokens),
            columns(tokens),
            columns(row_count),
            columns(row_count),
            whole,
        ],
        out_shape=[
            jax.ShapeDtypeStruct((tokens, width), BF),
            jax.ShapeDtypeStruct((tokens, width), BF),
            jax.ShapeDtypeStruct((row_count, width), BF),
            jax.ShapeDtypeStruct((row_count, width), BF),
            jax.ShapeDtypeStruct((row_count, enc), BF),
        ],
        scratch_shapes=[pltpu.VMEM((row_count, enc), F32)],
        compiler_params=pltpu.CompilerParams(
            vmem_limit_bytes=VMEM_LIMIT, dimension_semantics=("arbitrary",)
        ),
    )(flags, rows, key_w, value_w, queries, cotangent)


def weight_body(place, rows, rows_other, grads, grads_other, mine, away, total):
    pieces, height, _ = away.shape
    total[...] = dot(rows[...], grads[...], TN) + dot(rows_other[...], grads_other[...], TN)
    y = place[0]
    for k in range(pieces + 1):
        start = pl.multiple_of(lax.rem(y + k, pieces + 1) * height, 8)
        piece = total[pl.ds(start, height), :]
        if k == 0:
            mine[...] = piece
        else:
            away[k - 1] = piece.astype(BF)


def weight_grad(place, rows, rows_other, grads, grads_other, parts):
    row_count, enc = rows.shape
    width = grads.shape[1]
    block = 512
    height = enc // parts
    columns = pl.BlockSpec((row_count, block), lambda i: (0, i))
    whole = pl.BlockSpec((row_count, enc), lambda i: (0, 0))
    return pl.pallas_call(
        weight_body,
        grid=(width // block,),
        in_specs=[pl.BlockSpec(memory_space=pltpu.SMEM), whole, whole, columns, columns],
        out_specs=[
            pl.BlockSpec((height, block), lambda i: (0, i)),
            pl.BlockSpec((parts - 1, height, block), lambda i: (0, 0, i)),
        ],
        out_shape=[
            jax.ShapeDtypeStruct((height, width), F32),
            jax.ShapeDtypeStruct((parts - 1, height, width), BF),
        ],
        scratch_shapes=[pltpu.VMEM((enc, block), F32)],
        compiler_params=pltpu.CompilerParams(
            vmem_limit_bytes=VMEM_LIMIT, dimension_semantics=("arbitrary",)
        ),
    )(place, rows, rows_other, grads, grads_other)


def fold_body(place, mine, *refs):
    arrived, (own, away) = refs[:-2], refs[-2:]
    pieces, padded, width = away.shape
    height = own.shape[0]
    z = place[1]
    total = mine[...]
    for a in arrived:
        total = total + a[...].astype(F32)
    pad = jnp.zeros((padded - height, width), F32)
    for j in range(pieces + 1):
        piece = total[j * height : (j + 1) * height]
        slot = lax.rem(j - z + pieces + 1, pieces + 1)

        @pl.when(slot == 0)
        def _():
            own[...] = piece

        @pl.when(slot != 0)
        def _():
            away[slot - 1] = jnp.concatenate([piece, pad], axis=0).astype(BF)


def fold(place, mine, arrived, parts):
    height, width = mine.shape[0] // parts, mine.shape[1]
    vmem = pl.BlockSpec(memory_space=pltpu.VMEM)
    return pl.pallas_call(
        fold_body,
        in_specs=[pl.BlockSpec(memory_space=pltpu.SMEM)] + [vmem] * (1 + len(arrived)),
        out_specs=[vmem, vmem],
        out_shape=[
            jax.ShapeDtypeStruct((height, width), F32),
            jax.ShapeDtypeStruct((parts - 1, 32, width), BF),
        ],
        compiler_params=pltpu.CompilerParams(vmem_limit_bytes=VMEM_LIMIT),
    )(place, mine, *arrived)


def shards(queries, cotangent, neighbours, present, key_weight, value_weight):
    stretch_count, neigh_count, group, enc = neighbours.shape
    ny, nz, nx = 4, 8, 4
    y, z, core = lax.axis_index("y"), lax.axis_index("z"), lax.axis_index("c")
    place = jnp.stack([y, z])
    flags = jnp.concatenate([core[None], present.reshape(-1)]).astype(jnp.int32)
    swap = [(0, 1), (1, 0)]

    slab = neighbours.reshape(stretch_count, neigh_count * group, enc)
    slabs = [slab] + [lax.ppermute(slab, "x", ring(nx, k)) for k in (1, 3, 2)]
    rows = jnp.stack(slabs, axis=1).reshape(-1, enc)
    rows_other = lax.ppermute(rows, "c", swap)

    attended, query_grad, keep, send, passage = attend(
        flags, rows, key_weight, value_weight, queries, cotangent, stretch_count, group
    )
    grads_other = lax.ppermute(send, "c", swap)

    passage = passage.reshape(stretch_count, nx, neigh_count * group, enc)
    returned = [lax.ppermute(passage[:, s], "x", ring(nx, k)) for s, k in ((1, 3), (2, 1), (3, 2))]
    neighbour_grad = passage[:, 0].astype(F32)
    for r in returned:
        neighbour_grad = neighbour_grad + r.astype(F32)
    neighbour_grad = neighbour_grad.reshape(neighbours.shape)

    mine, away = weight_grad(place, rows, rows_other, keep, grads_other, ny)
    arrived = [lax.ppermute(away[k - 1], "y", ring(ny, k)) for k in (2, 1, 3)]
    own, further = fold(place, mine, arrived, nz)
    height = own.shape[0]
    summed = own
    for k in (4, 3, 5, 2, 6, 1, 7):
        summed = summed + lax.ppermute(further[k - 1], "z", ring(nz, k))[:height].astype(F32)
    half = height // 2
    low, high = summed[:half], summed[half:]
    first = core == 0
    other = lax.ppermute(jnp.where(first, high, low), "c", swap)
    stay = jnp.where(first, low, high)
    return (
        attended,
        query_grad,
        neighbour_grad,
        jnp.where(first, stay, other),
        jnp.where(first, other, stay),
    )


def solution(mesh):
    mesh = Mesh(mesh.devices.reshape(4, 8, 2, 4), ("y", "z", "c", "x"))
    dp = ("y", "z", "c")
    placed = (
        P(dp, "x"),
        P(dp, "x"),
        P(dp, None, "x", None),
        P(dp, None),
        P(None, "x"),
        P(None, "x"),
    )
    return jax.shard_map(
        shards,
        mesh=mesh,
        in_specs=placed,
        out_specs=(
            P(dp, "x"),
            P(dp, "x"),
            P(dp, None, "x", None),
            P(dp, "x"),
            P(dp, "x"),
        ),
        check_vma=False,
    )
```

```python
import jax
import jax.numpy as jnp
from jax import lax
from jax.experimental import pallas as pl
from jax.experimental.pallas import tpu as pltpu
from jax.sharding import Mesh, PartitionSpec as P

HEAD = 128
PAD = 32
BLOCK = 256
BF = jnp.bfloat16
F32 = jnp.float32
NN = (((1,), (0,)), ((), ()))
NT = (((1,), (1,)), ((), ()))
TN = (((0,), (0,)), ((), ()))
SMEM = pl.BlockSpec(memory_space=pltpu.SMEM)
VMEM = pl.BlockSpec(memory_space=pltpu.VMEM)
HBM = pl.BlockSpec(memory_space=pltpu.HBM)


def params(**more):
    return pltpu.CompilerParams(vmem_limit_bytes=32 * 1024 * 1024, **more)


def shape(dims, dtype):
    return pltpu.VMEM(dims, dtype)


def near_by(*arrays):
    return [pltpu.with_memory_space_constraint(a, pltpu.VMEM) for a in arrays]


def dot(a, b, dims=NN):
    return lax.dot_general(a, b, dims, preferred_element_type=F32)


def cost(flops, moved):
    return pl.CostEstimate(flops=flops, bytes_accessed=moved, transcendentals=0)


def hop(value, axis, size, step):
    inner = axis == "x"
    number = lambda i, core: core * size + i if inner else i * 2 + core
    pairs = []
    for core in range(2):
        for i in range(size):
            target = (i + (step if core == 0 else -step)) % size
            pairs.append((number(i, core), number(target, core)))
    return lax.ppermute(value, ("c", axis) if inner else (axis, "c"), pairs)


def swap(value):
    return lax.ppermute(value, "c", [(0, 1), (1, 0)])


def attention(q, g, k, v, live, empty):
    scale = HEAD ** (-0.5)
    tokens = q.shape[0]
    raw = jnp.exp(dot(q, k, NT) * scale) * live
    prob_grad = dot(g, v, NT)
    total = jnp.sum(raw, axis=-1, keepdims=True) + empty
    probs = raw * (1.0 / total)
    delta = jnp.sum(probs * prob_grad, axis=-1, keepdims=True)
    low = probs.astype(BF)
    score_grad = (probs * (prob_grad - delta) * scale).astype(BF)
    across = dot(jnp.concatenate([low, score_grad], axis=0), jnp.concatenate([v, k], axis=1))
    none = jnp.zeros_like(q)
    tall = jnp.concatenate(
        [jnp.concatenate([q, none], axis=1), jnp.concatenate([none, g], axis=1)], axis=0
    )
    down = dot(jnp.concatenate([score_grad, low], axis=0), tall, TN)
    return (
        across[:tokens, :HEAD].astype(BF),
        across[tokens:, HEAD:].astype(BF),
        down[:, :HEAD].astype(BF),
        down[:, HEAD:].astype(BF),
    )


def gathered(slabs, rows, offset):
    stretches, neigh, group, _ = slabs[0].shape
    first = offset
    for c in range(stretches):
        for s in slabs:
            for n in range(neigh):
                rows[first : first + group] = s[c, n]
                first += group


def load_body(*refs):
    count = (len(refs) - 1) // 2
    copies = [
        pltpu.make_async_copy(refs[i], refs[count + i], refs[-1].at[i]) for i in range(count)
    ]
    for copy in copies:
        copy.start()
    for copy in copies:
        copy.wait()


def load(*arrays):
    return pl.pallas_call(
        load_body,
        in_specs=[HBM] * len(arrays),
        out_specs=[VMEM] * len(arrays),
        out_shape=[shape(a.shape, a.dtype) for a in arrays],
        scratch_shapes=[pltpu.SemaphoreType.DMA((len(arrays),))],
        compiler_params=params(),
    )(*[pltpu.with_memory_space_constraint(a, pltpu.HBM) for a in arrays])


def attend_body(flags, s0, s1, s2, s3, key_w, value_w, queries, cotangent,
                attended, query_grad, keep, send, rows):
    stretches, neigh_count, group, _ = s0.shape
    span = 4 * neigh_count * group
    tokens = queries.shape[0] // stretches
    gathered((s0, s1, s2, s3), rows, 0)
    first = flags[0] == 0
    neigh = (lax.broadcasted_iota(jnp.int32, (1, span), 1) // group) % 2
    for start in range(0, queries.shape[1], BLOCK):
        here = slice(start, start + BLOCK)
        keys = dot(rows[...], key_w[:, here]).astype(BF)
        values = dot(rows[...], value_w[:, here]).astype(BF)
        for c in range(stretches):
            one, two = flags[1 + 2 * c], flags[2 + 2 * c]
            live = jnp.where(neigh == 0, one, two).astype(F32)
            empty = jnp.where(one + two == 0, 1.0, 0.0).astype(F32)
            r = slice(c * span, (c + 1) * span)
            t = slice(c * tokens, (c + 1) * tokens)
            for h in range(0, BLOCK, HEAD):
                w = slice(start + h, start + h + HEAD)
                out, q_grad, k_grad, v_grad = attention(
                    queries[t, w], cotangent[t, w],
                    keys[r, h : h + HEAD], values[r, h : h + HEAD], live, empty,
                )
                attended[t, w] = out
                query_grad[t, w] = q_grad
                keep[r, w] = jnp.where(first, k_grad, v_grad)
                send[r, w] = jnp.where(first, v_grad, k_grad)


def attend(flags, slabs, key_w, value_w, queries, cotangent):
    enc = slabs[0].shape[-1]
    row_count = 4 * slabs[0].size // enc
    tokens, width = queries.shape
    return pl.pallas_call(
        attend_body,
        in_specs=[SMEM] + [VMEM] * 8,
        out_specs=[VMEM] * 4,
        out_shape=[jax.ShapeDtypeStruct((tokens, width), BF)] * 2
        + [shape((row_count, width), BF)] * 2,
        scratch_shapes=[pltpu.VMEM((row_count, enc), BF)],
        compiler_params=params(),
        cost_estimate=cost(4 * 10**9, 5 * 10**6),
    )(flags, *near_by(*slabs, key_w, value_w, queries, cotangent))


def passage_body(flags, keep, send, key_hbm, value_hbm, o0, o1, o2, o3, key_w, value_w, sems):
    first = flags[0] == 0
    width = keep.shape[1]
    loads = []
    for i, start in enumerate(range(0, width, BLOCK)):
        here = pl.ds(start, BLOCK)
        for k, (source, target) in enumerate(((key_hbm, key_w), (value_hbm, value_w))):
            copy = pltpu.make_async_copy(source.at[:, here], target.at[i], sems.at[2 * i + k])
            copy.start()
            loads.append(copy)
    total = 0.0
    for i, start in enumerate(range(0, width, BLOCK)):
        a, b = keep[:, start : start + BLOCK], send[:, start : start + BLOCK]
        loads[2 * i].wait()
        loads[2 * i + 1].wait()
        total = total + dot(jnp.where(first, a, b), key_w[i], NT)
        total = total + dot(jnp.where(first, b, a), value_w[i], NT)
    stretches, neigh, group, _ = o0.shape
    start = 0
    for c in range(stretches):
        for o in (o0, o1, o2, o3):
            for n in range(neigh):
                o[c, n] = total[start : start + group].astype(o.dtype)
                start += group


def passage_grad(flags, keep, send, key_w, value_w, slab):
    enc, width = key_w.shape
    parts = width // BLOCK
    far = [pltpu.with_memory_space_constraint(a, pltpu.HBM) for a in (key_w, value_w)]
    return pl.pallas_call(
        passage_body,
        in_specs=[SMEM] + [VMEM] * 2 + [HBM] * 2,
        out_specs=[VMEM] * 4,
        out_shape=[shape(slab, d) for d in (F32, BF, F32, BF)],
        scratch_shapes=[
            pltpu.VMEM((parts, enc, BLOCK), BF),
            pltpu.VMEM((parts, enc, BLOCK), BF),
            pltpu.SemaphoreType.DMA((2 * parts,)),
        ],
        compiler_params=params(),
        cost_estimate=cost(4 * 10**9, 10**7),
    )(flags, *near_by(keep, send), *far)


def weight_body(a0, a1, a2, a3, grads, out, rows):
    gathered((a0, a1, a2, a3), rows, 0)
    out[...] = dot(rows[...], grads[...], TN)


def weight_grad(slabs, grads):
    enc = slabs[0].shape[-1]
    row_count, width = grads.shape
    return pl.pallas_call(
        weight_body,
        in_specs=[VMEM] * 5,
        out_specs=VMEM,
        out_shape=shape((enc, width), F32),
        scratch_shapes=[pltpu.VMEM((row_count, enc), BF)],
        compiler_params=params(),
        cost_estimate=cost(2 * 10**9, 5 * 10**6),
    )(*near_by(*slabs, grads))


def split_body(place, a0, a1, a2, a3, grads, partial, mine, far, back, front, rows, total):
    height = mine.shape[0]
    gathered((a0, a1, a2, a3), rows, 0)
    total[...] = partial[...] + dot(rows[...], grads[...], TN)
    for i, out in enumerate((mine, far, back, front)):
        first = pl.multiple_of(place[i] * height, 8)
        out[...] = total[pl.ds(first, height), :].astype(out.dtype)


def weight_split(place, slabs, grads, partial, parts):
    enc, width = partial.shape
    row_count = grads.shape[0]
    height = enc // parts
    return pl.pallas_call(
        split_body,
        in_specs=[SMEM] + [VMEM] * 6,
        out_specs=[VMEM] * 4,
        out_shape=[
            shape((height, width), F32),
            shape((height, width), BF),
            shape((height, width), BF),
            shape((height, width), F32),
        ],
        scratch_shapes=[pltpu.VMEM((row_count, enc), BF), pltpu.VMEM((enc, width), F32)],
        compiler_params=params(),
        cost_estimate=cost(2 * 10**9, 5 * 10**6),
    )(place, *near_by(*slabs, grads, partial))


def add_body(*refs):
    count = len(refs) // 3
    for i in range(count):
        total = refs[2 * i][...] + refs[2 * i + 1][...].astype(F32)
        refs[2 * count + i][...] = total.astype(BF)


def add(*pairs):
    return pl.pallas_call(
        add_body,
        in_specs=[VMEM] * (2 * len(pairs)),
        out_specs=[VMEM] * len(pairs),
        out_shape=[shape(a.shape, BF) for a, _ in pairs],
        compiler_params=params(),
    )(*near_by(*(a for pair in pairs for a in pair)))


def fold_body(place, mine, back, front, own, one, two, three, cross):
    height = own.shape[0]
    z, core = place[4], place[5]
    total = mine[...] + back[...].astype(F32) + front[...].astype(F32)
    pad = jnp.zeros((PAD - height, total.shape[1]), F32)
    for j in range(8):
        piece = total[j * height : (j + 1) * height]
        full = jnp.concatenate([piece, pad], axis=0)
        slot = lax.rem(jnp.where(core == 0, j - z, z - j) + 8, 8)

        @pl.when(slot == 0)
        def _():
            own[...] = piece

        @pl.when(slot == 1)
        def _():
            one[...] = full

        @pl.when(slot == 2)
        def _():
            two[...] = full

        @pl.when(slot == 3)
        def _():
            three[0] = full.astype(BF)

        @pl.when(slot == 4)
        def _():
            three[1] = full.astype(BF)

        for at, name in enumerate((7, 6, 5)):
            @pl.when(slot == name)
            def _():
                cross[at] = full.astype(BF)


def fold(place, mine, back, front):
    height, width = mine.shape[0] // 8, mine.shape[1]
    return pl.pallas_call(
        fold_body,
        in_specs=[SMEM] + [VMEM] * 3,
        out_specs=[VMEM] * 5,
        out_shape=[
            shape((height, width), F32),
            shape((PAD, width), F32),
            shape((PAD, width), F32),
            shape((2, PAD, width), BF),
            shape((3, PAD, width), BF),
        ],
        compiler_params=params(),
    )(place, *near_by(mine, back, front))


def pack_body(three, cross, out):
    out[:2] = three[...]
    out[2] = cross[2]


def pack(three, cross):
    return pl.pallas_call(
        pack_body,
        in_specs=[VMEM] * 2,
        out_specs=VMEM,
        out_shape=shape((3,) + three.shape[1:], BF),
        compiler_params=params(),
    )(*near_by(three, cross))


def relay_body(one, two, cross, arrived, to_one, to_two):
    to_one[0] = (one[...] + arrived[0].astype(F32)).astype(BF)
    to_one[1] = (cross[0].astype(F32) + arrived[2].astype(F32)).astype(BF)
    to_two[0] = (two[...] + arrived[1].astype(F32)).astype(BF)
    to_two[1] = cross[1]


def relay(one, two, cross, arrived):
    return pl.pallas_call(
        relay_body,
        in_specs=[VMEM] * 4,
        out_specs=[VMEM] * 2,
        out_shape=[shape((2,) + one.shape, BF)] * 2,
        compiler_params=params(),
    )(*near_by(one, two, cross, arrived))


def finish_body(place, own, one, two, stay, give):
    first = place[5] == 0
    height = own.shape[0]
    half = height // 2
    for k in range(2):
        value = (one[k].astype(F32) + two[k].astype(F32))[:height]
        if k == 0:
            value = value + own[...]
        low, high = value[:half], value[half:]
        stay[k] = jnp.where(first, low, high)
        give[k] = jnp.where(first, high, low)


def finish(place, own, one, two):
    height, width = own.shape
    dims = (2, height // 2, width)
    return pl.pallas_call(
        finish_body,
        in_specs=[SMEM] + [VMEM] * 3,
        out_specs=[VMEM] * 2,
        out_shape=[shape(dims, F32)] * 2,
        compiler_params=params(),
    )(place, *near_by(own, one, two))


def shards(queries, cotangent, neighbours, present, key_weight, value_weight):
    ny, nz, nx = 4, 8, 4
    y, z, core = lax.axis_index("y"), lax.axis_index("z"), lax.axis_index("c")
    first = core == 0
    sign = 1 - 2 * core
    place = jnp.stack([y, (y + 2) % ny, (y - sign) % ny, (y + sign) % ny, z, core])
    flags = jnp.concatenate([core[None], present.reshape(-1)]).astype(jnp.int32)
    tie = lax.optimization_barrier

    own = neighbours
    opposite = hop(own, "x", nx, 2)
    slabs = [own, hop(own, "x", nx, 1), hop(own, "x", nx, -1), opposite]
    others = [swap(s) for s in slabs]
    flags, place, start = tie((flags, place, own))
    loaded = load(key_weight, value_weight, queries, cotangent, start)
    slabs, loaded, others[0], others[3] = tie((slabs, loaded, others[0], others[3]))
    *loaded, slabs[0] = loaded

    attended, query_grad, keep, send = attend(flags, slabs, *loaded)
    received = swap(send)
    partial = weight_grad(slabs, keep)
    received, partial = tie((received, partial))
    mine, far, back, front = weight_split(place, others, received, partial, ny)
    far_in = hop(far, "y", ny, 1)
    keep, send, front = tie((keep, send, front))
    p0, p1, p2, p3 = passage_grad(flags, keep, send, key_weight, value_weight, own.shape)
    back_in = hop(back, "y", ny, -1)
    far_in, back_in, p1, p2, p3 = tie((far_in, back_in, p1, p2, p3))
    (front,) = add((front, far_in))
    front_in = hop(front, "y", ny, 1)
    front_in, beyond = tie((front_in, hop(p3, "x", nx, 1)))

    here, one, two, three, cross = fold(place, mine, back_in, front_in)
    cross = swap(cross)
    (share,) = add((p2, beyond))
    arrived = hop(pack(three, cross), "z", nz, 2)
    returned = [hop(p1, "x", nx, -1), hop(share, "x", nx, 1)]
    arrived, returned = tie((arrived, returned))
    one, two = relay(one, two, cross, arrived)
    stay, give = finish(place, here, hop(one, "z", nz, 1), hop(two, "z", nz, 2))
    other = swap(give)
    neighbour_grad = p0
    for r in returned:
        neighbour_grad = neighbour_grad + r.astype(F32)
    main, rest = stay[0] + other[1], stay[1] + other[0]
    return (
        attended,
        query_grad,
        neighbour_grad,
        jnp.where(first, main, rest),
        jnp.where(first, rest, main),
    )


def solution(mesh):
    mesh = Mesh(mesh.devices.reshape(4, 8, 2, 4), ("y", "z", "c", "x"))
    dp = ("y", "z", "c")
    placed = (
        P(dp, "x"),
        P(dp, "x"),
        P(dp, None, "x", None),
        P(dp, None),
        P(None, "x"),
        P(None, "x"),
    )
    return jax.shard_map(
        shards,
        mesh=mesh,
        in_specs=placed,
        out_specs=(
            P(dp, "x"),
            P(dp, "x"),
            P(dp, None, "x", None),
            P(dp, "x"),
            P(dp, "x"),
        ),
        check_vma=False,
    )
```

```python
import jax
import jax.numpy as jnp
from jax import lax
from jax.experimental import pallas as pl
from jax.experimental.pallas import tpu as pltpu
from jax.sharding import Mesh, PartitionSpec as P

HEAD = 128
PAD = 32
BLOCK = 512
BF = jnp.bfloat16
F32 = jnp.float32
NN = (((1,), (0,)), ((), ()))
NT = (((1,), (1,)), ((), ()))
TN = (((0,), (0,)), ((), ()))
SMEM = pl.BlockSpec(memory_space=pltpu.SMEM)
VMEM = pl.BlockSpec(memory_space=pltpu.VMEM)
HBM = pl.BlockSpec(memory_space=pltpu.HBM)


def params(**more):
    return pltpu.CompilerParams(vmem_limit_bytes=32 * 1024 * 1024, **more)


def shape(dims, dtype):
    return pltpu.VMEM(dims, dtype)


def near_by(*arrays):
    return [pltpu.with_memory_space_constraint(a, pltpu.VMEM) for a in arrays]


def dot(a, b, dims=NN):
    return lax.dot_general(a, b, dims, preferred_element_type=F32)


def cost(flops, moved):
    return pl.CostEstimate(flops=flops, bytes_accessed=moved, transcendentals=0)


def hop(value, axis, size, step, cross=False):
    inner = axis == "x"
    number = lambda i, core: core * size + i if inner else i * 2 + core
    pairs = []
    for core in range(2):
        for i in range(size):
            target = (i + (step if core == 0 else -step)) % size
            pairs.append((number(i, core), number(target, 1 - core if cross else core)))
    return lax.ppermute(value, ("c", axis) if inner else (axis, "c"), pairs)


def swap(value):
    return lax.ppermute(value, "c", [(0, 1), (1, 0)])


def scored(q, g, k, v, live, empty):
    scale = HEAD ** (-0.5)
    raw = jnp.exp(dot(q, k, NT) * scale) * live
    prob_grad = dot(g, v, NT)
    total = jnp.sum(raw, axis=-1, keepdims=True) + empty
    probs = raw * (1.0 / total)
    delta = jnp.sum(probs * prob_grad, axis=-1, keepdims=True)
    return probs.astype(BF), (probs * (prob_grad - delta) * scale).astype(BF)


def applied(q, g, k, v, low, score_grad):
    tokens = q.shape[0]
    across = dot(jnp.concatenate([low, score_grad], axis=0), jnp.concatenate([v, k], axis=1))
    none = jnp.zeros_like(q)
    tall = jnp.concatenate(
        [jnp.concatenate([q, none], axis=1), jnp.concatenate([none, g], axis=1)], axis=0
    )
    down = dot(jnp.concatenate([score_grad, low], axis=0), tall, TN)
    return (
        across[:tokens, :HEAD].astype(BF),
        across[tokens:, HEAD:].astype(BF),
        down[:, :HEAD].astype(BF),
        down[:, HEAD:].astype(BF),
    )


def gathered(slabs, rows, offset):
    stretches, neigh, group, _ = slabs[0].shape
    first = offset
    for c in range(stretches):
        for s in slabs:
            for n in range(neigh):
                rows[first : first + group] = s[c, n]
                first += group


def load_body(*refs):
    count = (len(refs) - 1) // 2
    copies = [
        pltpu.make_async_copy(refs[i], refs[count + i], refs[-1].at[i]) for i in range(count)
    ]
    for copy in copies:
        copy.start()
    for copy in copies:
        copy.wait()


def load(*arrays):
    return pl.pallas_call(
        load_body,
        in_specs=[HBM] * len(arrays),
        out_specs=[VMEM] * len(arrays),
        out_shape=[shape(a.shape, a.dtype) for a in arrays],
        scratch_shapes=[pltpu.SemaphoreType.DMA((len(arrays),))],
        compiler_params=params(),
    )(*[pltpu.with_memory_space_constraint(a, pltpu.HBM) for a in arrays])


def project_body(a, b, key_w, value_w, keys, values, rows):
    stretches, neigh_count, group, _ = a.shape
    gathered((a, b), rows, 0)
    span = 2 * neigh_count * group
    for weight, out in ((key_w, keys), (value_w, values)):
        done = dot(rows[...], weight[...]).astype(BF)
        for c in range(stretches):
            out[c] = done[c * span : (c + 1) * span]


def project(slabs, key_w, value_w):
    stretches, neigh_count, group, enc = slabs[0].shape
    dims = (stretches, 2 * neigh_count * group, key_w.shape[1])
    return pl.pallas_call(
        project_body,
        in_specs=[VMEM] * 4,
        out_specs=[VMEM] * 2,
        out_shape=[shape(dims, BF)] * 2,
        scratch_shapes=[pltpu.VMEM((stretches * dims[1], enc), BF)],
        compiler_params=params(),
    )(*near_by(*slabs, key_w, value_w))


def attend_body(group, flags, k1, v1, k2, v2, queries, cotangent,
                attended, query_grad, keep, send):
    stretches, half, width = k1.shape
    span = 2 * half
    tokens = queries.shape[0] // stretches
    first = flags[0] == 0
    neigh = (lax.broadcasted_iota(jnp.int32, (1, span), 1) // group) % 2
    masks = []
    for c in range(stretches):
        one, two = flags[1 + 2 * c], flags[2 + 2 * c]
        live = jnp.where(neigh == 0, one, two).astype(F32)
        masks.append((live, jnp.where(one + two == 0, 1.0, 0.0).astype(F32)))
    for start in range(0, width, BLOCK):
        waiting = []
        for c in range(stretches):
            r = slice(c * span, (c + 1) * span)
            t = slice(c * tokens, (c + 1) * tokens)
            for h in range(start, start + BLOCK, HEAD):
                w = slice(h, h + HEAD)
                heads = (
                    queries[t, w], cotangent[t, w],
                    jnp.concatenate([k1[c, :, w], k2[c, :, w]], axis=0),
                    jnp.concatenate([v1[c, :, w], v2[c, :, w]], axis=0),
                )
                waiting.append((r, t, w, heads, scored(*heads, *masks[c])))
        for r, t, w, heads, scores in waiting:
            out, q_grad, k_grad, v_grad = applied(*heads, *scores)
            attended[t, w] = out
            query_grad[t, w] = q_grad
            keep[r, w] = jnp.where(first, k_grad, v_grad)
            send[r, w] = jnp.where(first, v_grad, k_grad)


def attend(flags, k1, v1, k2, v2, queries, cotangent, group):
    stretches, half, width = k1.shape
    tokens = queries.shape[0]
    row_count = 2 * stretches * half
    return pl.pallas_call(
        lambda *refs: attend_body(group, *refs),
        in_specs=[SMEM] + [VMEM] * 6,
        out_specs=[VMEM] * 4,
        out_shape=[jax.ShapeDtypeStruct((tokens, width), BF)] * 2
        + [shape((row_count, width), BF)] * 2,
        compiler_params=params(),
    )(flags, *near_by(k1, v1, k2, v2, queries, cotangent))


def passage_body(flags, keep, send, key_hbm, value_hbm, o0, o1, o2, o3, key_w, value_w, sems):
    first = flags[0] == 0
    width = keep.shape[1]
    loads = []
    for i, start in enumerate(range(0, width, BLOCK)):
        here = pl.ds(start, BLOCK)
        for k, (source, target) in enumerate(((key_hbm, key_w), (value_hbm, value_w))):
            copy = pltpu.make_async_copy(source.at[:, here], target.at[i], sems.at[2 * i + k])
            copy.start()
            loads.append(copy)
    total = 0.0
    for i, start in enumerate(range(0, width, BLOCK)):
        a, b = keep[:, start : start + BLOCK], send[:, start : start + BLOCK]
        loads[2 * i].wait()
        loads[2 * i + 1].wait()
        total = total + dot(jnp.where(first, a, b), key_w[i], NT)
        total = total + dot(jnp.where(first, b, a), value_w[i], NT)
    stretches, neigh, group, _ = o0.shape
    start = 0
    for c in range(stretches):
        for o in (o0, o1, o2, o3):
            for n in range(neigh):
                o[c, n] = total[start : start + group].astype(o.dtype)
                start += group


def passage_grad(flags, keep, send, key_w, value_w, slab):
    enc, width = key_w.shape
    parts = width // BLOCK
    far = [pltpu.with_memory_space_constraint(a, pltpu.HBM) for a in (key_w, value_w)]
    return pl.pallas_call(
        passage_body,
        in_specs=[SMEM] + [VMEM] * 2 + [HBM] * 2,
        out_specs=[VMEM] * 4,
        out_shape=[shape(slab, d) for d in (F32, BF, BF, F32)],
        scratch_shapes=[
            pltpu.VMEM((parts, enc, BLOCK), BF),
            pltpu.VMEM((parts, enc, BLOCK), BF),
            pltpu.SemaphoreType.DMA((2 * parts,)),
        ],
        compiler_params=params(),
        cost_estimate=cost(4 * 10**9, 10**7),
    )(flags, *near_by(keep, send), *far)


def weight_body(a0, a1, a2, a3, grads, out, rows):
    gathered((a0, a1, a2, a3), rows, 0)
    out[...] = dot(rows[...], grads[...], TN)


def weight_grad(slabs, grads):
    enc = slabs[0].shape[-1]
    row_count, width = grads.shape
    return pl.pallas_call(
        weight_body,
        in_specs=[VMEM] * 5,
        out_specs=VMEM,
        out_shape=shape((enc, width), F32),
        scratch_shapes=[pltpu.VMEM((row_count, enc), BF)],
        compiler_params=params(),
        cost_estimate=cost(2 * 10**9, 5 * 10**6),
    )(*near_by(*slabs, grads))


def split_body(place, a0, a1, a2, a3, grads, partial, mine, far, back, front, rows, total):
    height = mine.shape[0]
    gathered((a0, a1, a2, a3), rows, 0)
    total[...] = partial[...] + dot(rows[...], grads[...], TN)
    for i, out in enumerate((mine, far, back, front)):
        first = pl.multiple_of(place[i] * height, 8)
        out[...] = total[pl.ds(first, height), :].astype(out.dtype)


def weight_split(place, slabs, grads, partial, parts):
    enc, width = partial.shape
    row_count = grads.shape[0]
    height = enc // parts
    return pl.pallas_call(
        split_body,
        in_specs=[SMEM] + [VMEM] * 6,
        out_specs=[VMEM] * 4,
        out_shape=[
            shape((height, width), F32),
            shape((height, width), BF),
            shape((height, width), BF),
            shape((height, width), F32),
        ],
        scratch_shapes=[pltpu.VMEM((row_count, enc), BF), pltpu.VMEM((enc, width), F32)],
        compiler_params=params(),
        cost_estimate=cost(2 * 10**9, 5 * 10**6),
    )(place, *near_by(*slabs, grads, partial))


def add_body(a, b, out):
    out[...] = (a[...] + b[...].astype(F32)).astype(BF)


def add(a, b):
    return pl.pallas_call(
        add_body,
        in_specs=[VMEM] * 2,
        out_specs=VMEM,
        out_shape=shape(a.shape, BF),
        compiler_params=params(),
    )(*near_by(a, b))


def deal_body(place, a, b, c, d, front, front_cross, base, base_cross):
    z, core = place[4], place[5]
    height = a.shape[0] // 8
    pad = jnp.zeros((PAD - height, a.shape[1]), F32)
    total = a[...] + b[...].astype(F32)
    rest = c[...] + d[...].astype(F32)
    for j in range(8):
        rows = slice(j * height, (j + 1) * height)
        one = jnp.concatenate([total[rows], pad], axis=0).astype(BF)
        two = jnp.concatenate([rest[rows], pad], axis=0)
        slot = lax.rem(jnp.where(core == 0, j - z, z - j) + 8, 8)

        @pl.when(slot < 5)
        def _():
            front[slot] = one
            base[slot] = two

        @pl.when(slot > 4)
        def _():
            front_cross[7 - slot] = one
            base_cross[7 - slot] = two


def deal(place, front, far_in, mine, back_in):
    width = mine.shape[1]
    return pl.pallas_call(
        deal_body,
        in_specs=[SMEM] + [VMEM] * 4,
        out_specs=[VMEM] * 4,
        out_shape=[shape((n, PAD, width), dtype) for dtype in (BF, F32) for n in (5, 3)],
        compiler_params=params(),
    )(place, *near_by(front, far_in, mine, back_in))


def fold_body(base, front, cross, front_cross, own, one, two, three):
    height = own.shape[0]
    add_up = lambda a, b, i: a[i] + b[i].astype(F32)
    own[...] = add_up(base, front, 0)[:height]
    one[0] = add_up(base, front, 1).astype(BF)
    one[1] = add_up(base, front, 4).astype(BF)
    one[2] = add_up(cross, front_cross, 0).astype(BF)
    two[0] = add_up(base, front, 2).astype(BF)
    two[1] = add_up(cross, front_cross, 1).astype(BF)
    three[0] = add_up(base, front, 3)
    three[1] = add_up(cross, front_cross, 2)


def fold(base, front, cross, front_cross, height):
    _, pad, width = base.shape
    return pl.pallas_call(
        fold_body,
        in_specs=[VMEM] * 4,
        out_specs=[VMEM] * 4,
        out_shape=[
            shape((height, width), F32),
            shape((3, pad, width), BF),
            shape((2, pad, width), BF),
            shape((2, pad, width), F32),
        ],
        compiler_params=params(),
    )(*near_by(base, front, cross, front_cross))


def relay_body(three, arrived, out):
    out[0] = (three[0] + arrived[1].astype(F32)).astype(BF)
    out[1] = three[1].astype(BF)


def relay(three, arrived):
    return pl.pallas_call(
        relay_body,
        in_specs=[VMEM] * 2,
        out_specs=VMEM,
        out_shape=shape(three.shape, BF),
        compiler_params=params(),
    )(*near_by(three, arrived))


def finish_body(place, own, one, two, three, stay, give):
    first = place[5] == 0
    height = own.shape[0]
    half = height // 2
    for k in range(2):
        value = one[2 * k].astype(F32) + two[k].astype(F32) + three[k].astype(F32)
        value = value[:height]
        if k == 0:
            value = value + own[...]
        low, high = value[:half], value[half:]
        stay[k] = jnp.where(first, low, high)
        give[k] = jnp.where(first, high, low)


def finish(place, own, one, two, three):
    height, width = own.shape
    dims = (2, height // 2, width)
    return pl.pallas_call(
        finish_body,
        in_specs=[SMEM] + [VMEM] * 4,
        out_specs=[VMEM] * 2,
        out_shape=[shape(dims, F32)] * 2,
        compiler_params=params(),
    )(place, *near_by(own, one, two, three))


def shards(queries, cotangent, neighbours, present, key_weight, value_weight):
    ny, nz, nx = 4, 8, 4
    y, z, core = lax.axis_index("y"), lax.axis_index("z"), lax.axis_index("c")
    first = core == 0
    sign = 1 - 2 * core
    place = jnp.stack([y, (y + 2) % ny, (y - sign) % ny, (y + sign) % ny, z, core])
    flags = jnp.concatenate([core[None], present.reshape(-1)]).astype(jnp.int32)
    tie = lax.optimization_barrier

    own = neighbours
    opposite, behind, ahead = (hop(own, "x", nx, step) for step in (2, 1, -1))
    flags, place, start = tie((flags, place, own))
    key_w, value_w, q, g, own = load(key_weight, value_weight, queries, cotangent, start)
    opposite, own = tie((opposite, own))
    k1, v1 = project((own, opposite), key_w, value_w)
    others = [swap(neighbours), swap(opposite)]
    behind, ahead, k1, v1, *others = tie((behind, ahead, k1, v1, *others))
    k2, v2 = project((behind, ahead), key_w, value_w)
    others += [swap(behind), swap(ahead)]
    k2, *others = tie((k2, *others))
    slabs = (own, opposite, behind, ahead)

    attended, query_grad, keep, send = attend(flags, k1, v1, k2, v2, q, g, own.shape[2])
    received = swap(send)
    partial = weight_grad(slabs, keep)
    received, partial = tie((received, partial))
    mine, far, back, front = weight_split(place, others, received, partial, ny)
    far_in = hop(far, "y", ny, 1)
    keep, send, front = tie((keep, send, front))
    p0, p3, p1, p2 = passage_grad(flags, keep, send, key_weight, value_weight, own.shape)
    back_in = hop(back, "y", ny, -1)
    far_in, back_in, p1, p2, p3 = tie((far_in, back_in, p1, p2, p3))
    front, front_cross, base, cross = deal(place, front, far_in, mine, back_in)
    front_in = hop(front, "y", ny, 1)
    cross_in = hop(front_cross, "y", ny, 1, cross=True)
    cross = swap(cross)
    front_in, cross_in, beyond = tie((front_in, cross_in, hop(p3, "x", nx, 1)))
    p1_in = hop(p1, "x", nx, -1)

    here, one, two, three = fold(base, front_in, cross, cross_in, mine.shape[0] // nz)
    one_in = hop(one, "z", nz, 1)
    two_in = hop(two, "z", nz, 2)
    three_in = hop(relay(three, one_in), "z", nz, 3)
    share = add(p2, beyond)
    returned = [p1_in, hop(share, "x", nx, 1)]
    three_in, returned = tie((three_in, returned))
    stay, give = finish(place, here, one_in, two_in, three_in)
    other = swap(give)
    neighbour_grad = p0
    for r in returned:
        neighbour_grad = neighbour_grad + r.astype(F32)
    main, rest = stay[0] + other[1], stay[1] + other[0]
    return (
        attended,
        query_grad,
        neighbour_grad,
        jnp.where(first, main, rest),
        jnp.where(first, rest, main),
    )


def solution(mesh):
    mesh = Mesh(mesh.devices.reshape(4, 8, 2, 4), ("y", "z", "c", "x"))
    dp = ("y", "z", "c")
    placed = (
        P(dp, "x"),
        P(dp, "x"),
        P(dp, None, "x", None),
        P(dp, None),
        P(None, "x"),
        P(None, "x"),
    )
    return jax.shard_map(
        shards,
        mesh=mesh,
        in_specs=placed,
        out_specs=(
            P(dp, "x"),
            P(dp, "x"),
            P(dp, None, "x", None),
            P(dp, "x"),
            P(dp, "x"),
        ),
        check_vma=False,
    )
```

```python
import jax
import jax.numpy as jnp
from jax import lax
from jax.experimental import pallas as pl
from jax.experimental.pallas import tpu as pltpu
from jax.sharding import Mesh, PartitionSpec as P

HEAD = 128
PAD = 32
BLOCK = 512
BF = jnp.bfloat16
F32 = jnp.float32
NN = (((1,), (0,)), ((), ()))
NT = (((1,), (1,)), ((), ()))
TN = (((0,), (0,)), ((), ()))
SMEM = pl.BlockSpec(memory_space=pltpu.SMEM)
VMEM = pl.BlockSpec(memory_space=pltpu.VMEM)
HBM = pl.BlockSpec(memory_space=pltpu.HBM)


def params(**more):
    return pltpu.CompilerParams(vmem_limit_bytes=32 * 1024 * 1024, **more)


def shape(dims, dtype):
    return pltpu.VMEM(dims, dtype)


def near_by(*arrays):
    return [pltpu.with_memory_space_constraint(a, pltpu.VMEM) for a in arrays]


def dot(a, b, dims=NN):
    return lax.dot_general(a, b, dims, preferred_element_type=F32)


def cost(flops, moved):
    return pl.CostEstimate(flops=flops, bytes_accessed=moved, transcendentals=0)


def hop(value, axis, size, step, cross=False):
    inner = axis == "x"
    number = lambda i, core: core * size + i if inner else i * 2 + core
    pairs = []
    for core in range(2):
        for i in range(size):
            target = (i + (step if core == 0 else -step)) % size
            pairs.append((number(i, core), number(target, 1 - core if cross else core)))
    return lax.ppermute(value, ("c", axis) if inner else (axis, "c"), pairs)


def swap(value):
    return lax.ppermute(value, "c", [(0, 1), (1, 0)])


def scored(q, g, k, v, live, empty):
    scale = HEAD ** (-0.5)
    raw = jnp.exp(dot(q, k, NT) * scale) * live
    prob_grad = dot(g, v, NT)
    total = jnp.sum(raw, axis=-1, keepdims=True) + empty
    probs = raw * (1.0 / total)
    delta = jnp.sum(probs * prob_grad, axis=-1, keepdims=True)
    return probs.astype(BF), (probs * (prob_grad - delta) * scale).astype(BF)


def applied(q, g, k, v, low, score_grad):
    tokens = q.shape[0]
    across = dot(jnp.concatenate([low, score_grad], axis=0), jnp.concatenate([v, k], axis=1))
    none = jnp.zeros_like(q)
    tall = jnp.concatenate(
        [jnp.concatenate([q, none], axis=1), jnp.concatenate([none, g], axis=1)], axis=0
    )
    down = dot(jnp.concatenate([score_grad, low], axis=0), tall, TN)
    return (
        across[:tokens, :HEAD].astype(BF),
        across[tokens:, HEAD:].astype(BF),
        down[:, :HEAD].astype(BF),
        down[:, HEAD:].astype(BF),
    )


def gathered(slabs, rows, offset):
    stretches, neigh, group, _ = slabs[0].shape
    first = offset
    for c in range(stretches):
        for s in slabs:
            for n in range(neigh):
                rows[first : first + group] = s[c, n]
                first += group


def load_body(*refs):
    count = (len(refs) - 1) // 2
    copies = [
        pltpu.make_async_copy(refs[i], refs[count + i], refs[-1].at[i]) for i in range(count)
    ]
    for copy in copies:
        copy.start()
    for copy in copies:
        copy.wait()


def load(*arrays):
    return pl.pallas_call(
        load_body,
        in_specs=[HBM] * len(arrays),
        out_specs=[VMEM] * len(arrays),
        out_shape=[shape(a.shape, a.dtype) for a in arrays],
        scratch_shapes=[pltpu.SemaphoreType.DMA((len(arrays),))],
        compiler_params=params(),
    )(*[pltpu.with_memory_space_constraint(a, pltpu.HBM) for a in arrays])


def project_body(a, b, key_w, value_w, keys, values, rows):
    stretches, neigh_count, group, _ = a.shape
    gathered((a, b), rows, 0)
    span = 2 * neigh_count * group
    for weight, out in ((key_w, keys), (value_w, values)):
        done = dot(rows[...], weight[...]).astype(BF)
        for c in range(stretches):
            out[c] = done[c * span : (c + 1) * span]


def project(slabs, key_w, value_w):
    stretches, neigh_count, group, enc = slabs[0].shape
    dims = (stretches, 2 * neigh_count * group, key_w.shape[1])
    return pl.pallas_call(
        project_body,
        in_specs=[VMEM] * 4,
        out_specs=[VMEM] * 2,
        out_shape=[shape(dims, BF)] * 2,
        scratch_shapes=[pltpu.VMEM((stretches * dims[1], enc), BF)],
        compiler_params=params(),
    )(*near_by(*slabs, key_w, value_w))


def attend_body(group, flags, k1, v1, k2, v2, queries, cotangent,
                attended, query_grad, keep, send):
    stretches, half, width = k1.shape
    span = 2 * half
    tokens = queries.shape[0] // stretches
    first = flags[0] == 0
    neigh = (lax.broadcasted_iota(jnp.int32, (1, span), 1) // group) % 2
    masks = []
    for c in range(stretches):
        one, two = flags[1 + 2 * c], flags[2 + 2 * c]
        live = jnp.where(neigh == 0, one, two).astype(F32)
        masks.append((live, jnp.where(one + two == 0, 1.0, 0.0).astype(F32)))
    for start in range(0, width, BLOCK):
        waiting = []
        for c in range(stretches):
            r = slice(c * span, (c + 1) * span)
            t = slice(c * tokens, (c + 1) * tokens)
            for h in range(start, start + BLOCK, HEAD):
                w = slice(h, h + HEAD)
                heads = (
                    queries[t, w], cotangent[t, w],
                    jnp.concatenate([k1[c, :, w], k2[c, :, w]], axis=0),
                    jnp.concatenate([v1[c, :, w], v2[c, :, w]], axis=0),
                )
                waiting.append((r, t, w, heads, scored(*heads, *masks[c])))
        for r, t, w, heads, scores in waiting:
            out, q_grad, k_grad, v_grad = applied(*heads, *scores)
            attended[t, w] = out
            query_grad[t, w] = q_grad
            keep[r, w] = jnp.where(first, k_grad, v_grad)
            send[r, w] = jnp.where(first, v_grad, k_grad)


def attend(flags, k1, v1, k2, v2, queries, cotangent, group):
    stretches, half, width = k1.shape
    tokens = queries.shape[0]
    row_count = 2 * stretches * half
    return pl.pallas_call(
        lambda *refs: attend_body(group, *refs),
        in_specs=[SMEM] + [VMEM] * 6,
        out_specs=[VMEM] * 4,
        out_shape=[jax.ShapeDtypeStruct((tokens, width), BF)] * 2
        + [shape((row_count, width), BF)] * 2,
        compiler_params=params(),
    )(flags, *near_by(k1, v1, k2, v2, queries, cotangent))


def passage_body(flags, keep, send, key_hbm, value_hbm, o0, o1, o2, o3, key_w, value_w, sems):
    first = flags[0] == 0
    width = keep.shape[1]
    loads = []
    for i, start in enumerate(range(0, width, BLOCK)):
        here = pl.ds(start, BLOCK)
        for k, (source, target) in enumerate(((key_hbm, key_w), (value_hbm, value_w))):
            copy = pltpu.make_async_copy(source.at[:, here], target.at[i], sems.at[2 * i + k])
            copy.start()
            loads.append(copy)
    total = 0.0
    for i, start in enumerate(range(0, width, BLOCK)):
        a, b = keep[:, start : start + BLOCK], send[:, start : start + BLOCK]
        loads[2 * i].wait()
        loads[2 * i + 1].wait()
        total = total + dot(jnp.where(first, a, b), key_w[i], NT)
        total = total + dot(jnp.where(first, b, a), value_w[i], NT)
    stretches, neigh, group, _ = o0.shape
    start = 0
    for c in range(stretches):
        for o in (o0, o1, o2, o3):
            for n in range(neigh):
                o[c, n] = total[start : start + group].astype(o.dtype)
                start += group


def passage_grad(flags, keep, send, key_w, value_w, slab):
    enc, width = key_w.shape
    parts = width // BLOCK
    far = [pltpu.with_memory_space_constraint(a, pltpu.HBM) for a in (key_w, value_w)]
    return pl.pallas_call(
        passage_body,
        in_specs=[SMEM] + [VMEM] * 2 + [HBM] * 2,
        out_specs=[VMEM] * 4,
        out_shape=[shape(slab, d) for d in (F32, BF, BF, F32)],
        scratch_shapes=[
            pltpu.VMEM((parts, enc, BLOCK), BF),
            pltpu.VMEM((parts, enc, BLOCK), BF),
            pltpu.SemaphoreType.DMA((2 * parts,)),
        ],
        compiler_params=params(),
        cost_estimate=cost(4 * 10**9, 10**7),
    )(flags, *near_by(keep, send), *far)


def weight_body(a0, a1, a2, a3, grads, out, rows):
    gathered((a0, a1, a2, a3), rows, 0)
    out[...] = dot(rows[...], grads[...], TN)


def weight_grad(slabs, grads):
    enc = slabs[0].shape[-1]
    row_count, width = grads.shape
    return pl.pallas_call(
        weight_body,
        in_specs=[VMEM] * 5,
        out_specs=VMEM,
        out_shape=shape((enc, width), F32),
        scratch_shapes=[pltpu.VMEM((row_count, enc), BF)],
        compiler_params=params(),
        cost_estimate=cost(2 * 10**9, 5 * 10**6),
    )(*near_by(*slabs, grads))


def split_body(place, a0, a1, a2, a3, grads, partial, mine, far, back, front, rows, total):
    height = mine.shape[0]
    gathered((a0, a1, a2, a3), rows, 0)
    total[...] = partial[...] + dot(rows[...], grads[...], TN)
    for i, out in enumerate((mine, far, back, front)):
        first = pl.multiple_of(place[i] * height, 8)
        out[...] = total[pl.ds(first, height), :].astype(out.dtype)


def weight_split(place, slabs, grads, partial, parts):
    enc, width = partial.shape
    row_count = grads.shape[0]
    height = enc // parts
    return pl.pallas_call(
        split_body,
        in_specs=[SMEM] + [VMEM] * 6,
        out_specs=[VMEM] * 4,
        out_shape=[
            shape((height, width), F32),
            shape((height, width), BF),
            shape((height, width), BF),
            shape((height, width), F32),
        ],
        scratch_shapes=[pltpu.VMEM((row_count, enc), BF), pltpu.VMEM((enc, width), F32)],
        compiler_params=params(),
        cost_estimate=cost(2 * 10**9, 5 * 10**6),
    )(place, *near_by(*slabs, grads, partial))


def add_body(a, b, out):
    out[...] = (a[...] + b[...].astype(F32)).astype(BF)


def add(a, b):
    return pl.pallas_call(
        add_body,
        in_specs=[VMEM] * 2,
        out_specs=VMEM,
        out_shape=shape(a.shape, BF),
        compiler_params=params(),
    )(*near_by(a, b))


def deal_body(place, a, b, ours, theirs):
    z, core = place[4], place[5]
    total = a[...] + b[...].astype(F32)
    height = total.shape[0] // 8
    pad = jnp.zeros((PAD - height, total.shape[1]), F32)
    for j in range(8):
        piece = jnp.concatenate([total[j * height : (j + 1) * height], pad], axis=0)
        slot = lax.rem(jnp.where(core == 0, j - z, z - j) + 8, 8)

        @pl.when(slot < 5)
        def _():
            ours[slot] = piece.astype(ours.dtype)

        @pl.when(slot > 4)
        def _():
            theirs[7 - slot] = piece.astype(theirs.dtype)


def deal(place, a, b, dtype):
    width = a.shape[1]
    return pl.pallas_call(
        deal_body,
        in_specs=[SMEM] + [VMEM] * 2,
        out_specs=[VMEM] * 2,
        out_shape=[shape((5, PAD, width), dtype), shape((3, PAD, width), BF)],
        compiler_params=params(),
        cost_estimate=cost(0, 0),
    )(place, *near_by(a, b))


def fold_body(base, front, cross, front_cross, own, one, two, three):
    height = own.shape[0]
    add_up = lambda a, b, i: a[i].astype(F32) + b[i].astype(F32)
    own[...] = add_up(base, front, 0)[:height]
    one[0] = add_up(base, front, 1).astype(BF)
    one[1] = add_up(base, front, 4).astype(BF)
    one[2] = add_up(cross, front_cross, 0).astype(BF)
    two[0] = add_up(base, front, 2).astype(BF)
    two[1] = add_up(cross, front_cross, 1).astype(BF)
    three[0] = add_up(base, front, 3)
    three[1] = add_up(cross, front_cross, 2)


def fold(base, front, cross, front_cross, height):
    _, pad, width = base.shape
    return pl.pallas_call(
        fold_body,
        in_specs=[VMEM] * 4,
        out_specs=[VMEM] * 4,
        out_shape=[
            shape((height, width), F32),
            shape((3, pad, width), BF),
            shape((2, pad, width), BF),
            shape((2, pad, width), F32),
        ],
        compiler_params=params(),
    )(*near_by(base, front, cross, front_cross))


def relay_body(three, arrived, out):
    out[0] = (three[0] + arrived[1].astype(F32)).astype(BF)
    out[1] = three[1].astype(BF)


def relay(three, arrived):
    return pl.pallas_call(
        relay_body,
        in_specs=[VMEM] * 2,
        out_specs=VMEM,
        out_shape=shape(three.shape, BF),
        compiler_params=params(),
    )(*near_by(three, arrived))


def finish_body(place, own, one, two, three, stay, give):
    first = place[5] == 0
    height = own.shape[0]
    half = height // 2
    for k in range(2):
        value = one[2 * k].astype(F32) + two[k].astype(F32) + three[k].astype(F32)
        value = value[:height]
        if k == 0:
            value = value + own[...]
        low, high = value[:half], value[half:]
        stay[k] = jnp.where(first, low, high)
        give[k] = jnp.where(first, high, low)


def finish(place, own, one, two, three):
    height, width = own.shape
    dims = (2, height // 2, width)
    return pl.pallas_call(
        finish_body,
        in_specs=[SMEM] + [VMEM] * 4,
        out_specs=[VMEM] * 2,
        out_shape=[shape(dims, F32)] * 2,
        compiler_params=params(),
        cost_estimate=pl.CostEstimate(flops=2 * 10**10, bytes_accessed=4 * 10**7, transcendentals=0),
    )(place, *near_by(own, one, two, three))


def shards(queries, cotangent, neighbours, present, key_weight, value_weight):
    ny, nz, nx = 4, 8, 4
    y, z, core = lax.axis_index("y"), lax.axis_index("z"), lax.axis_index("c")
    first = core == 0
    sign = 1 - 2 * core
    place = jnp.stack([y, (y + 2) % ny, (y - sign) % ny, (y + sign) % ny, z, core])
    flags = jnp.concatenate([core[None], present.reshape(-1)]).astype(jnp.int32)
    tie = lax.optimization_barrier

    own = neighbours
    opposite, behind, ahead = (hop(own, "x", nx, step) for step in (2, 1, -1))
    flags, place, start = tie((flags, place, own))
    key_w, value_w, q, g, own = load(key_weight, value_weight, queries, cotangent, start)
    opposite, own = tie((opposite, own))
    k1, v1 = project((own, opposite), key_w, value_w)
    others = [swap(neighbours), swap(opposite)]
    behind, ahead, k1, v1, *others = tie((behind, ahead, k1, v1, *others))
    k2, v2 = project((behind, ahead), key_w, value_w)
    others += [swap(behind), swap(ahead)]
    k2, *others = tie((k2, *others))
    slabs = (own, opposite, behind, ahead)

    attended, query_grad, keep, send = attend(flags, k1, v1, k2, v2, q, g, own.shape[2])
    received = swap(send)
    partial = weight_grad(slabs, keep)
    received, partial = tie((received, partial))
    mine, far, back, front = weight_split(place, others, received, partial, ny)
    far_in = hop(far, "y", ny, 1)
    keep, send, front = tie((keep, send, front))
    p0, p3, p1, p2 = passage_grad(flags, keep, send, key_weight, value_weight, own.shape)
    back, p1, p2, p3 = tie((back, p1, p2, p3))
    back_in = hop(back, "y", ny, -1)
    front, front_cross = deal(place, front, far_in, BF)
    front, front_cross, mine = tie((front, front_cross, mine))
    front_in = hop(front, "y", ny, 1)
    cross_in = hop(front_cross, "y", ny, 1, cross=True)
    base, cross = deal(place, mine, back_in, F32)
    cross = swap(cross)
    front_in, cross_in, beyond = tie((front_in, cross_in, hop(p3, "x", nx, 1)))

    here, one, two, three = fold(base, front_in, cross, cross_in, mine.shape[0] // nz)
    one_in = hop(one, "z", nz, 1)
    two_in = hop(two, "z", nz, 2)
    share = add(p2, beyond)
    three, share, p1 = tie((relay(three, one_in), share, p1))
    three_in = hop(three, "z", nz, 3)
    returned = [hop(p1, "x", nx, -1), hop(share, "x", nx, 1)]
    stay, give = finish(place, here, one_in, two_in, three_in)
    other = swap(give)
    neighbour_grad = p0
    for r in returned:
        neighbour_grad = neighbour_grad + r.astype(F32)
    main, rest = stay[0] + other[1], stay[1] + other[0]
    return (
        attended,
        query_grad,
        neighbour_grad,
        jnp.where(first, main, rest),
        jnp.where(first, rest, main),
    )


def solution(mesh):
    mesh = Mesh(mesh.devices.reshape(4, 8, 2, 4), ("y", "z", "c", "x"))
    dp = ("y", "z", "c")
    placed = (
        P(dp, "x"),
        P(dp, "x"),
        P(dp, None, "x", None),
        P(dp, None),
        P(None, "x"),
        P(None, "x"),
    )
    return jax.shard_map(
        shards,
        mesh=mesh,
        in_specs=placed,
        out_specs=(
            P(dp, "x"),
            P(dp, "x"),
            P(dp, None, "x", None),
            P(dp, "x"),
            P(dp, "x"),
        ),
        check_vma=False,
    )
```

```python
import jax
import jax.numpy as jnp
from jax import lax
from jax.experimental import pallas as pl
from jax.experimental.pallas import tpu as pltpu
from jax.sharding import Mesh, PartitionSpec as P

HEAD = 128
PAD = 32
BLOCK = 512
PART = 256
BF = jnp.bfloat16
F32 = jnp.float32
NN = (((1,), (0,)), ((), ()))
NT = (((1,), (1,)), ((), ()))
TN = (((0,), (0,)), ((), ()))
SMEM = pl.BlockSpec(memory_space=pltpu.SMEM)
VMEM = pl.BlockSpec(memory_space=pltpu.VMEM)
HBM = pl.BlockSpec(memory_space=pltpu.HBM)


def params(**more):
    return pltpu.CompilerParams(vmem_limit_bytes=32 * 1024 * 1024, **more)


def shape(dims, dtype):
    return pltpu.VMEM(dims, dtype)


def near_by(*arrays):
    return [pltpu.with_memory_space_constraint(a, pltpu.VMEM) for a in arrays]


def dot(a, b, dims=NN):
    return lax.dot_general(a, b, dims, preferred_element_type=F32)


def cost(flops, moved):
    return pl.CostEstimate(flops=flops, bytes_accessed=moved, transcendentals=0)


def hop(value, axis, size, step, cross=False):
    inner = axis == "x"
    number = lambda i, core: core * size + i if inner else i * 2 + core
    pairs = []
    for core in range(2):
        for i in range(size):
            target = (i + (step if core == 0 else -step)) % size
            pairs.append((number(i, core), number(target, 1 - core if cross else core)))
    return lax.ppermute(value, ("c", axis) if inner else (axis, "c"), pairs)


def swap(value):
    return lax.ppermute(value, "c", [(0, 1), (1, 0)])


def scored(q, g, k, v, live, empty):
    scale = HEAD ** (-0.5)
    raw = jnp.exp(dot(q, k, NT) * scale) * live
    prob_grad = dot(g, v, NT)
    total = jnp.sum(raw, axis=-1, keepdims=True) + empty
    probs = raw * (1.0 / total)
    delta = jnp.sum(probs * prob_grad, axis=-1, keepdims=True)
    return probs.astype(BF), (probs * (prob_grad - delta) * scale).astype(BF)


def applied(q, g, k, v, low, score_grad):
    tokens = q.shape[0]
    across = dot(jnp.concatenate([low, score_grad], axis=0), jnp.concatenate([v, k], axis=1))
    none = jnp.zeros_like(q)
    tall = jnp.concatenate(
        [jnp.concatenate([q, none], axis=1), jnp.concatenate([none, g], axis=1)], axis=0
    )
    down = dot(jnp.concatenate([score_grad, low], axis=0), tall, TN)
    return (
        across[:tokens, :HEAD].astype(BF),
        across[tokens:, HEAD:].astype(BF),
        down[:, :HEAD].astype(BF),
        down[:, HEAD:].astype(BF),
    )


def gathered(slabs, rows, offset):
    stretches, neigh, group, _ = slabs[0].shape
    first = offset
    for c in range(stretches):
        for s in slabs:
            for n in range(neigh):
                rows[first : first + group] = s[c, n]
                first += group


def load_body(*refs):
    count = (len(refs) - 1) // 2
    copies = [
        pltpu.make_async_copy(refs[i], refs[count + i], refs[-1].at[i]) for i in range(count)
    ]
    for copy in copies:
        copy.start()
    for copy in copies:
        copy.wait()


def load(*arrays):
    return pl.pallas_call(
        load_body,
        in_specs=[HBM] * len(arrays),
        out_specs=[VMEM] * len(arrays),
        out_shape=[shape(a.shape, a.dtype) for a in arrays],
        scratch_shapes=[pltpu.SemaphoreType.DMA((len(arrays),))],
        compiler_params=params(),
    )(*[pltpu.with_memory_space_constraint(a, pltpu.HBM) for a in arrays])


def project_body(a, b, key_w, value_w, keys, values, rows):
    stretches, neigh_count, group, _ = a.shape
    gathered((a, b), rows, 0)
    span = 2 * neigh_count * group
    for weight, out in ((key_w, keys), (value_w, values)):
        done = dot(rows[...], weight[...]).astype(BF)
        for c in range(stretches):
            out[c] = done[c * span : (c + 1) * span]


def project(slabs, key_w, value_w):
    stretches, neigh_count, group, enc = slabs[0].shape
    dims = (stretches, 2 * neigh_count * group, key_w.shape[1])
    return pl.pallas_call(
        project_body,
        in_specs=[VMEM] * 4,
        out_specs=[VMEM] * 2,
        out_shape=[shape(dims, BF)] * 2,
        scratch_shapes=[pltpu.VMEM((stretches * dims[1], enc), BF)],
        compiler_params=params(),
    )(*near_by(*slabs, key_w, value_w))


def attend_body(group, flags, k1, v1, k2, v2, queries, cotangent,
                attended, query_grad, keep, send):
    stretches, half, width = k1.shape
    span = 2 * half
    tokens = queries.shape[0] // stretches
    first = flags[0] == 0
    neigh = (lax.broadcasted_iota(jnp.int32, (1, span), 1) // group) % 2
    masks = []
    for c in range(stretches):
        one, two = flags[1 + 2 * c], flags[2 + 2 * c]
        live = jnp.where(neigh == 0, one, two).astype(F32)
        masks.append((live, jnp.where(one + two == 0, 1.0, 0.0).astype(F32)))
    for start in range(0, width, BLOCK):
        waiting = []
        for c in range(stretches):
            r = slice(c * span, (c + 1) * span)
            t = slice(c * tokens, (c + 1) * tokens)
            for h in range(start, start + BLOCK, HEAD):
                w = slice(h, h + HEAD)
                heads = (
                    queries[t, w], cotangent[t, w],
                    jnp.concatenate([k1[c, :, w], k2[c, :, w]], axis=0),
                    jnp.concatenate([v1[c, :, w], v2[c, :, w]], axis=0),
                )
                waiting.append((r, t, w, heads, scored(*heads, *masks[c])))
        for r, t, w, heads, scores in waiting:
            out, q_grad, k_grad, v_grad = applied(*heads, *scores)
            attended[t, w] = out
            query_grad[t, w] = q_grad
            keep[r, w] = jnp.where(first, k_grad, v_grad)
            send[r, w] = jnp.where(first, v_grad, k_grad)


def attend(flags, k1, v1, k2, v2, queries, cotangent, group):
    stretches, half, width = k1.shape
    tokens = queries.shape[0]
    row_count = 2 * stretches * half
    return pl.pallas_call(
        lambda *refs: attend_body(group, *refs),
        in_specs=[SMEM] + [VMEM] * 6,
        out_specs=[VMEM] * 4,
        out_shape=[jax.ShapeDtypeStruct((tokens, width), BF)] * 2
        + [shape((row_count, width), BF)] * 2,
        compiler_params=params(),
    )(flags, *near_by(k1, v1, k2, v2, queries, cotangent))


def passage_add(flags, keep, send, total, columns, weights):
    first = flags[0] == 0
    for (key_w, value_w), start in zip(weights, columns):
        a, b = keep[:, start : start + PART], send[:, start : start + PART]
        total = total + dot(jnp.where(first, a, b), key_w[...], NT)
        total = total + dot(jnp.where(first, b, a), value_w[...], NT)
    return total


def passage_open_body(flags, keep, send, key_hbm, value_hbm, partial, *refs):
    parts = keep.shape[1] // PART
    rest, (key_w, value_w, sems) = refs[: 2 * parts - 2], refs[2 * parts - 2 :]
    targets = (key_w, value_w) + rest
    loads = [
        pltpu.make_async_copy(
            (key_hbm, value_hbm)[i % 2].at[:, pl.ds(i // 2 * PART, PART)], target, sems.at[i]
        )
        for i, target in enumerate(targets)
    ]
    for load in loads:
        load.start()
    for load in loads[:2]:
        load.wait()
    partial[...] = passage_add(flags, keep, send, 0.0, (0,), ((key_w, value_w),))
    for load in loads[2:]:
        load.wait()


def passage_open(flags, keep, send, key_w, value_w):
    enc, width = key_w.shape
    rest = 2 * (width // PART) - 2
    far = [pltpu.with_memory_space_constraint(a, pltpu.HBM) for a in (key_w, value_w)]
    return pl.pallas_call(
        passage_open_body,
        in_specs=[SMEM] + [VMEM] * 2 + [HBM] * 2,
        out_specs=[VMEM] * (1 + rest),
        out_shape=[shape((keep.shape[0], enc), F32)] + [shape((enc, PART), BF)] * rest,
        scratch_shapes=[
            pltpu.VMEM((enc, PART), BF),
            pltpu.VMEM((enc, PART), BF),
            pltpu.SemaphoreType.DMA((rest + 2,)),
        ],
        compiler_params=params(),
        cost_estimate=cost(2 * 10**9, 5 * 10**6),
    )(flags, *near_by(keep, send), *far)


def passage_close_body(flags, keep, send, partial, *refs):
    rest, outs = refs[:-4], refs[-4:]
    pairs = list(zip(rest[::2], rest[1::2]))
    columns = range(PART, keep.shape[1], PART)
    total = passage_add(flags, keep, send, partial[...], columns, pairs)
    stretches, neigh, group, _ = outs[0].shape
    start = 0
    for c in range(stretches):
        for o in outs:
            for n in range(neigh):
                o[c, n] = total[start : start + group].astype(o.dtype)
                start += group


def passage_close(flags, keep, send, partial, rest, slab):
    return pl.pallas_call(
        passage_close_body,
        in_specs=[SMEM] + [VMEM] * (3 + len(rest)),
        out_specs=[VMEM] * 4,
        out_shape=[shape(slab, d) for d in (F32, BF, BF, F32)],
        compiler_params=params(),
        cost_estimate=cost(2 * 10**9, 5 * 10**6),
    )(flags, *near_by(keep, send, partial, *rest))


def weight_body(a0, a1, a2, a3, b0, b1, b2, b3, grads, out, turned, rows):
    gathered((b0, b1, b2, b3), rows, 0)
    turned[...] = rows[...].T
    gathered((a0, a1, a2, a3), rows, 0)
    out[...] = dot(rows[...], grads[...], TN)


def weight_grad(slabs, slabs_other, grads):
    enc = slabs[0].shape[-1]
    row_count, width = grads.shape
    return pl.pallas_call(
        weight_body,
        in_specs=[VMEM] * 9,
        out_specs=[VMEM] * 2,
        out_shape=[shape((enc, width), F32), shape((enc, row_count), BF)],
        scratch_shapes=[pltpu.VMEM((row_count, enc), BF)],
        compiler_params=params(),
        cost_estimate=cost(2 * 10**9, 5 * 10**6),
    )(*near_by(*slabs, *slabs_other, grads))


def split_body(which, place, turned, grads, partial, *outs):
    for i, out in zip(which, outs):
        height = out.shape[0]
        here = pl.ds(pl.multiple_of(place[i] * height, 32), height)
        total = partial[here, :] + dot(turned[here, :], grads[...])
        out[...] = total.astype(out.dtype)


def weight_split(place, turned, grads, partial, parts, which, dtypes):
    enc, width = partial.shape
    return pl.pallas_call(
        lambda *refs: split_body(which, *refs),
        in_specs=[SMEM] + [VMEM] * 3,
        out_specs=[VMEM] * len(which),
        out_shape=[shape((enc // parts, width), d) for d in dtypes],
        compiler_params=params(),
        cost_estimate=cost(10**9, 5 * 10**6),
    )(place, *near_by(turned, grads, partial))


def add_body(a, b, out):
    out[...] = (a[...] + b[...].astype(F32)).astype(BF)


def add(a, b):
    return pl.pallas_call(
        add_body,
        in_specs=[VMEM] * 2,
        out_specs=VMEM,
        out_shape=shape(a.shape, BF),
        compiler_params=params(),
    )(*near_by(a, b))


def deal_body(place, a, b, ours, theirs):
    z, core = place[4], place[5]
    total = a[...] + b[...].astype(F32)
    height = total.shape[0] // 8
    pad = jnp.zeros((PAD - height, total.shape[1]), F32)
    for j in range(8):
        piece = jnp.concatenate([total[j * height : (j + 1) * height], pad], axis=0)
        slot = lax.rem(jnp.where(core == 0, j - z, z - j) + 8, 8)

        @pl.when(slot < 5)
        def _():
            ours[slot] = piece.astype(ours.dtype)

        @pl.when(slot > 4)
        def _():
            theirs[7 - slot] = piece.astype(theirs.dtype)


def deal(place, a, b, dtype):
    width = a.shape[1]
    return pl.pallas_call(
        deal_body,
        in_specs=[SMEM] + [VMEM] * 2,
        out_specs=[VMEM] * 2,
        out_shape=[shape((5, PAD, width), dtype), shape((3, PAD, width), BF)],
        compiler_params=params(),
        cost_estimate=cost(0, 0),
    )(place, *near_by(a, b))


def fold_body(base, front, cross, front_cross, own, one, two, three):
    height = own.shape[0]
    add_up = lambda a, b, i: a[i].astype(F32) + b[i].astype(F32)
    own[...] = add_up(base, front, 0)[:height]
    one[0] = add_up(base, front, 1).astype(BF)
    one[1] = add_up(base, front, 4).astype(BF)
    one[2] = add_up(cross, front_cross, 0).astype(BF)
    two[0] = add_up(base, front, 2).astype(BF)
    two[1] = add_up(cross, front_cross, 1).astype(BF)
    three[0] = add_up(base, front, 3)
    three[1] = add_up(cross, front_cross, 2)


def fold(base, front, cross, front_cross, height):
    _, pad, width = base.shape
    return pl.pallas_call(
        fold_body,
        in_specs=[VMEM] * 4,
        out_specs=[VMEM] * 4,
        out_shape=[
            shape((height, width), F32),
            shape((3, pad, width), BF),
            shape((2, pad, width), BF),
            shape((2, pad, width), F32),
        ],
        compiler_params=params(),
    )(*near_by(base, front, cross, front_cross))


def relay_body(three, arrived, out):
    out[0] = (three[0] + arrived[1].astype(F32)).astype(BF)
    out[1] = three[1].astype(BF)


def relay(three, arrived):
    return pl.pallas_call(
        relay_body,
        in_specs=[VMEM] * 2,
        out_specs=VMEM,
        out_shape=shape(three.shape, BF),
        compiler_params=params(),
    )(*near_by(three, arrived))


def finish_body(place, own, one, two, three, stay, give):
    first = place[5] == 0
    height = own.shape[0]
    half = height // 2
    for k in range(2):
        value = one[2 * k].astype(F32) + two[k].astype(F32) + three[k].astype(F32)
        value = value[:height]
        if k == 0:
            value = value + own[...]
        low, high = value[:half], value[half:]
        stay[k] = jnp.where(first, low, high)
        give[k] = jnp.where(first, high, low)


def finish(place, own, one, two, three):
    height, width = own.shape
    dims = (2, height // 2, width)
    return pl.pallas_call(
        finish_body,
        in_specs=[SMEM] + [VMEM] * 4,
        out_specs=[VMEM] * 2,
        out_shape=[shape(dims, F32)] * 2,
        compiler_params=params(),
        cost_estimate=pl.CostEstimate(flops=2 * 10**10, bytes_accessed=4 * 10**7, transcendentals=0),
    )(place, *near_by(own, one, two, three))


def shards(queries, cotangent, neighbours, present, key_weight, value_weight):
    ny, nz, nx = 4, 8, 4
    y, z, core = lax.axis_index("y"), lax.axis_index("z"), lax.axis_index("c")
    first = core == 0
    sign = 1 - 2 * core
    place = jnp.stack([y, (y + 2) % ny, (y - sign) % ny, (y + sign) % ny, z, core])
    flags = jnp.concatenate([core[None], present.reshape(-1)]).astype(jnp.int32)
    tie = lax.optimization_barrier

    own = neighbours
    opposite, behind, ahead = (hop(own, "x", nx, step) for step in (2, 1, -1))
    flags, place, start = tie((flags, place, own))
    key_w, value_w, q, g, own = load(key_weight, value_weight, queries, cotangent, start)
    opposite, own = tie((opposite, own))
    k1, v1 = project((own, opposite), key_w, value_w)
    others = [swap(neighbours), swap(opposite)]
    behind, ahead, k1, v1, *others = tie((behind, ahead, k1, v1, *others))
    k2, v2 = project((behind, ahead), key_w, value_w)
    others += [swap(behind), swap(ahead)]
    k2, *others = tie((k2, *others))
    slabs = (own, opposite, behind, ahead)

    attended, query_grad, keep, send = attend(flags, k1, v1, k2, v2, q, g, own.shape[2])
    received = swap(send)
    partial, turned = weight_grad(slabs, others, keep)
    received, partial = tie((received, partial))
    (far,) = weight_split(place, turned, received, partial, ny, (1,), (BF,))
    far_in = hop(far, "y", ny, 1)
    far, partial = tie((far, partial))
    mine, back, front = weight_split(
        place, turned, received, partial, ny, (0, 2, 3), (F32, BF, F32)
    )
    keep, send, front = tie((keep, send, front))
    part, *rest = passage_open(flags, keep, send, key_weight, value_weight)
    back, part = tie((back, part))
    back_in = hop(back, "y", ny, -1)
    p0, p3, p1, p2 = passage_close(flags, keep, send, part, rest, own.shape)
    far_in, p1, p2, p3 = tie((far_in, p1, p2, p3))
    front, front_cross = deal(place, front, far_in, BF)
    front, front_cross, mine = tie((front, front_cross, mine))
    front_in = hop(front, "y", ny, 1)
    cross_in = hop(front_cross, "y", ny, 1, cross=True)
    base, cross = deal(place, mine, back_in, F32)
    cross = swap(cross)
    p1_in = hop(p1, "x", nx, -1)
    front_in, cross_in, beyond, p1_in = tie((front_in, cross_in, hop(p3, "x", nx, 1), p1_in))

    here, one, two, three = fold(base, front_in, cross, cross_in, mine.shape[0] // nz)
    one_in = hop(one, "z", nz, 1)
    two_in = hop(two, "z", nz, 2)
    share = add(p2, beyond)
    three, share = tie((relay(three, one_in), share))
    three_in = hop(three, "z", nz, 3)
    returned = [p1_in, hop(share, "x", nx, 1)]
    stay, give = finish(place, here, one_in, two_in, three_in)
    other = swap(give)
    neighbour_grad = p0
    for r in returned:
        neighbour_grad = neighbour_grad + r.astype(F32)
    main, rest = stay[0] + other[1], stay[1] + other[0]
    return (
        attended,
        query_grad,
        neighbour_grad,
        jnp.where(first, main, rest),
        jnp.where(first, rest, main),
    )


def solution(mesh):
    mesh = Mesh(mesh.devices.reshape(4, 8, 2, 4), ("y", "z", "c", "x"))
    dp = ("y", "z", "c")
    placed = (
        P(dp, "x"),
        P(dp, "x"),
        P(dp, None, "x", None),
        P(dp, None),
        P(None, "x"),
        P(None, "x"),
    )
    return jax.shard_map(
        shards,
        mesh=mesh,
        in_specs=placed,
        out_specs=(
            P(dp, "x"),
            P(dp, "x"),
            P(dp, None, "x", None),
            P(dp, "x"),
            P(dp, "x"),
        ),
        check_vma=False,
    )
```

```python
import jax
import jax.numpy as jnp
from jax import lax
from jax.experimental import pallas as pl
from jax.experimental.pallas import tpu as pltpu
from jax.sharding import Mesh, PartitionSpec as P

HEAD = 128
PAD = 32
BLOCK = 512
PART = 256
BF = jnp.bfloat16
F32 = jnp.float32
NN = (((1,), (0,)), ((), ()))
NT = (((1,), (1,)), ((), ()))
TN = (((0,), (0,)), ((), ()))
SMEM = pl.BlockSpec(memory_space=pltpu.SMEM)
VMEM = pl.BlockSpec(memory_space=pltpu.VMEM)
HBM = pl.BlockSpec(memory_space=pltpu.HBM)


def params(**more):
    return pltpu.CompilerParams(vmem_limit_bytes=32 * 1024 * 1024, **more)


def shape(dims, dtype):
    return pltpu.VMEM(dims, dtype)


def near_by(*arrays):
    return [pltpu.with_memory_space_constraint(a, pltpu.VMEM) for a in arrays]


def dot(a, b, dims=NN):
    return lax.dot_general(a, b, dims, preferred_element_type=F32)


def cost(flops, moved):
    return pl.CostEstimate(flops=flops, bytes_accessed=moved, transcendentals=0)


def position():
    y, z, core = lax.axis_index("y"), lax.axis_index("z"), lax.axis_index("c")
    sign = 1 - 2 * core
    return [y] + [lax.rem(y + 4 + by, 4) for by in (2, -sign, sign)] + [z, core]


def hop(value, axis, size, step, cross=False):
    inner = axis == "x"
    number = lambda i, core: core * size + i if inner else i * 2 + core
    pairs = []
    for core in range(2):
        for i in range(size):
            target = (i + (step if core == 0 else -step)) % size
            pairs.append((number(i, core), number(target, 1 - core if cross else core)))
    return lax.ppermute(value, ("c", axis) if inner else (axis, "c"), pairs)


def swap(value):
    return lax.ppermute(value, "c", [(0, 1), (1, 0)])


def scored(q, g, k, v, live, empty):
    scale = HEAD ** (-0.5)
    raw = jnp.exp(dot(q, k, NT) * scale) * live
    prob_grad = dot(g, v, NT)
    total = jnp.sum(raw, axis=-1, keepdims=True) + empty
    probs = raw * (1.0 / total)
    delta = jnp.sum(probs * prob_grad, axis=-1, keepdims=True)
    return probs.astype(BF), (probs * (prob_grad - delta) * scale).astype(BF)


def applied(q, g, k, v, low, score_grad):
    tokens = q.shape[0]
    across = dot(jnp.concatenate([low, score_grad], axis=0), jnp.concatenate([v, k], axis=1))
    none = jnp.zeros_like(q)
    tall = jnp.concatenate(
        [jnp.concatenate([q, none], axis=1), jnp.concatenate([none, g], axis=1)], axis=0
    )
    down = dot(jnp.concatenate([score_grad, low], axis=0), tall, TN)
    return (
        across[:tokens, :HEAD].astype(BF),
        across[tokens:, HEAD:].astype(BF),
        down[:, :HEAD].astype(BF),
        down[:, HEAD:].astype(BF),
    )


def gathered(slabs, rows, offset):
    stretches, neigh, group, _ = slabs[0].shape
    first = offset
    for c in range(stretches):
        for s in slabs:
            for n in range(neigh):
                rows[first : first + group] = s[c, n]
                first += group


def load_body(*refs):
    count = (len(refs) - 1) // 2
    copies = [
        pltpu.make_async_copy(refs[i], refs[count + i], refs[-1].at[i]) for i in range(count)
    ]
    for copy in copies:
        copy.start()
    for copy in copies:
        copy.wait()


def load(*arrays):
    return pl.pallas_call(
        load_body,
        in_specs=[HBM] * len(arrays),
        out_specs=[VMEM] * len(arrays),
        out_shape=[shape(a.shape, a.dtype) for a in arrays],
        scratch_shapes=[pltpu.SemaphoreType.DMA((len(arrays),))],
        compiler_params=params(),
    )(*[pltpu.with_memory_space_constraint(a, pltpu.HBM) for a in arrays])


def project_body(a, b, key_w, value_w, keys, values, rows):
    stretches, neigh_count, group, _ = a.shape
    gathered((a, b), rows, 0)
    span = 2 * neigh_count * group
    for weight, out in ((key_w, keys), (value_w, values)):
        done = dot(rows[...], weight[...]).astype(BF)
        for c in range(stretches):
            out[c] = done[c * span : (c + 1) * span]


def project(slabs, key_w, value_w):
    stretches, neigh_count, group, enc = slabs[0].shape
    dims = (stretches, 2 * neigh_count * group, key_w.shape[1])
    return pl.pallas_call(
        project_body,
        in_specs=[VMEM] * 4,
        out_specs=[VMEM] * 2,
        out_shape=[shape(dims, BF)] * 2,
        scratch_shapes=[pltpu.VMEM((stretches * dims[1], enc), BF)],
        compiler_params=params(),
    )(*near_by(*slabs, key_w, value_w))


def attend_body(group, flags, k1, v1, k2, v2, queries, cotangent,
                attended, query_grad, keep, send):
    stretches, half, width = k1.shape
    span = 2 * half
    tokens = queries.shape[0] // stretches
    first = flags[0] == 0
    neigh = (lax.broadcasted_iota(jnp.int32, (1, span), 1) // group) % 2
    masks = []
    for c in range(stretches):
        one, two = flags[1 + 2 * c], flags[2 + 2 * c]
        live = jnp.where(neigh == 0, one, two).astype(F32)
        masks.append((live, jnp.where(one + two == 0, 1.0, 0.0).astype(F32)))
    for start in range(0, width, BLOCK):
        waiting = []
        for c in range(stretches):
            r = slice(c * span, (c + 1) * span)
            t = slice(c * tokens, (c + 1) * tokens)
            for h in range(start, start + BLOCK, HEAD):
                w = slice(h, h + HEAD)
                heads = (
                    queries[t, w], cotangent[t, w],
                    jnp.concatenate([k1[c, :, w], k2[c, :, w]], axis=0),
                    jnp.concatenate([v1[c, :, w], v2[c, :, w]], axis=0),
                )
                waiting.append((r, t, w, heads, scored(*heads, *masks[c])))
        for r, t, w, heads, scores in waiting:
            out, q_grad, k_grad, v_grad = applied(*heads, *scores)
            attended[t, w] = out
            query_grad[t, w] = q_grad
            keep[r, w] = jnp.where(first, k_grad, v_grad)
            send[r, w] = jnp.where(first, v_grad, k_grad)


def attend(flags, k1, v1, k2, v2, queries, cotangent, group):
    stretches, half, width = k1.shape
    tokens = queries.shape[0]
    row_count = 2 * stretches * half
    return pl.pallas_call(
        lambda *refs: attend_body(group, *refs),
        in_specs=[SMEM] + [VMEM] * 6,
        out_specs=[VMEM] * 4,
        out_shape=[jax.ShapeDtypeStruct((tokens, width), BF)] * 2
        + [shape((row_count, width), BF)] * 2,
        compiler_params=params(),
    )(flags, *near_by(k1, v1, k2, v2, queries, cotangent))


def passage_add(keep, send, total, columns, weights):
    first = lax.axis_index("c") == 0
    for (key_w, value_w), start in zip(weights, columns):
        a, b = keep[:, start : start + PART], send[:, start : start + PART]
        total = total + dot(jnp.where(first, a, b), key_w[...], NT)
        total = total + dot(jnp.where(first, b, a), value_w[...], NT)
    return total


def passage_open_body(keep, send, key_hbm, value_hbm, partial, *refs):
    parts = keep.shape[1] // PART
    rest, (key_w, value_w, sems) = refs[: 2 * parts - 2], refs[2 * parts - 2 :]
    targets = (key_w, value_w) + rest
    loads = [
        pltpu.make_async_copy(
            (key_hbm, value_hbm)[i % 2].at[:, pl.ds(i // 2 * PART, PART)], target, sems.at[i]
        )
        for i, target in enumerate(targets)
    ]
    for load in loads:
        load.start()
    for load in loads[:2]:
        load.wait()
    partial[...] = passage_add(keep, send, 0.0, (0,), ((key_w, value_w),))
    for load in loads[2:]:
        load.wait()


def passage_open(keep, send, key_w, value_w):
    enc, width = key_w.shape
    rest = 2 * (width // PART) - 2
    far = [pltpu.with_memory_space_constraint(a, pltpu.HBM) for a in (key_w, value_w)]
    return pl.pallas_call(
        passage_open_body,
        in_specs=[VMEM] * 2 + [HBM] * 2,
        out_specs=[VMEM] * (1 + rest),
        out_shape=[shape((keep.shape[0], enc), F32)] + [shape((enc, PART), BF)] * rest,
        scratch_shapes=[
            pltpu.VMEM((enc, PART), BF),
            pltpu.VMEM((enc, PART), BF),
            pltpu.SemaphoreType.DMA((rest + 2,)),
        ],
        compiler_params=params(),
        cost_estimate=cost(2 * 10**9, 5 * 10**6),
    )(*near_by(keep, send), *far)


def passage_close_body(keep, send, partial, *refs):
    rest, outs = refs[:-4], refs[-4:]
    pairs = list(zip(rest[::2], rest[1::2]))
    columns = range(PART, keep.shape[1], PART)
    total = passage_add(keep, send, partial[...], columns, pairs)
    stretches, neigh, group, _ = outs[0].shape
    start = 0
    for c in range(stretches):
        for o in outs:
            for n in range(neigh):
                o[c, n] = total[start : start + group].astype(o.dtype)
                start += group


def passage_close(keep, send, partial, rest, slab):
    return pl.pallas_call(
        passage_close_body,
        in_specs=[VMEM] * (3 + len(rest)),
        out_specs=[VMEM] * 4,
        out_shape=[shape(slab, d) for d in (F32, BF, BF, F32)],
        compiler_params=params(),
        cost_estimate=cost(2 * 10**9, 5 * 10**6),
    )(*near_by(keep, send, partial, *rest))


def weight_body(a0, a1, a2, a3, b0, b1, b2, b3, grads, out, turned, rows):
    gathered((b0, b1, b2, b3), rows, 0)
    turned[...] = rows[...].T
    gathered((a0, a1, a2, a3), rows, 0)
    out[...] = dot(rows[...], grads[...], TN)


def weight_grad(slabs, slabs_other, grads):
    enc = slabs[0].shape[-1]
    row_count, width = grads.shape
    return pl.pallas_call(
        weight_body,
        in_specs=[VMEM] * 9,
        out_specs=[VMEM] * 2,
        out_shape=[shape((enc, width), F32), shape((enc, row_count), BF)],
        scratch_shapes=[pltpu.VMEM((row_count, enc), BF)],
        compiler_params=params(),
        cost_estimate=cost(2 * 10**9, 5 * 10**6),
    )(*near_by(*slabs, *slabs_other, grads))


def split_body(which, turned, grads, partial, *outs):
    place = position()
    for i, out in zip(which, outs):
        height = out.shape[0]
        here = pl.ds(pl.multiple_of(place[i] * height, 32), height)
        total = partial[here, :] + dot(turned[here, :], grads[...])
        out[...] = total.astype(out.dtype)


def weight_split(turned, grads, partial, parts, which, dtypes):
    enc, width = partial.shape
    return pl.pallas_call(
        lambda *refs: split_body(which, *refs),
        in_specs=[VMEM] * 3,
        out_specs=[VMEM] * len(which),
        out_shape=[shape((enc // parts, width), d) for d in dtypes],
        compiler_params=params(),
        cost_estimate=cost(10**9, 5 * 10**6),
    )(*near_by(turned, grads, partial))


def add_body(a, b, out):
    out[...] = (a[...] + b[...].astype(F32)).astype(BF)


def add(a, b):
    return pl.pallas_call(
        add_body,
        in_specs=[VMEM] * 2,
        out_specs=VMEM,
        out_shape=shape(a.shape, BF),
        compiler_params=params(),
    )(*near_by(a, b))


def deal_body(a, b, ours, theirs):
    z, core = position()[4:]
    total = a[...] + b[...].astype(F32)
    height = total.shape[0] // 8
    pad = jnp.zeros((PAD - height, total.shape[1]), F32)
    for j in range(8):
        piece = jnp.concatenate([total[j * height : (j + 1) * height], pad], axis=0)
        slot = lax.rem(jnp.where(core == 0, j - z, z - j) + 8, 8)

        @pl.when(slot < 5)
        def _():
            ours[slot] = piece.astype(ours.dtype)

        @pl.when(slot > 4)
        def _():
            theirs[7 - slot] = piece.astype(theirs.dtype)


def deal(a, b, dtype):
    width = a.shape[1]
    return pl.pallas_call(
        deal_body,
        in_specs=[VMEM] * 2,
        out_specs=[VMEM] * 2,
        out_shape=[shape((5, PAD, width), dtype), shape((3, PAD, width), BF)],
        compiler_params=params(),
        cost_estimate=cost(0, 0),
    )(*near_by(a, b))


def fold_body(base, front, cross, front_cross, own, one, two, three):
    height = own.shape[0]
    add_up = lambda a, b, i: a[i].astype(F32) + b[i].astype(F32)
    own[...] = add_up(base, front, 0)[:height]
    one[0] = add_up(base, front, 1).astype(BF)
    one[1] = add_up(base, front, 4).astype(BF)
    one[2] = add_up(cross, front_cross, 0).astype(BF)
    two[0] = add_up(base, front, 2).astype(BF)
    two[1] = add_up(cross, front_cross, 1).astype(BF)
    three[0] = add_up(base, front, 3)
    three[1] = add_up(cross, front_cross, 2)


def fold(base, front, cross, front_cross, height):
    _, pad, width = base.shape
    return pl.pallas_call(
        fold_body,
        in_specs=[VMEM] * 4,
        out_specs=[VMEM] * 4,
        out_shape=[
            shape((height, width), F32),
            shape((3, pad, width), BF),
            shape((2, pad, width), BF),
            shape((2, pad, width), F32),
        ],
        compiler_params=params(),
    )(*near_by(base, front, cross, front_cross))


def relay_body(three, arrived, out):
    out[0] = (three[0] + arrived[1].astype(F32)).astype(BF)
    out[1] = three[1].astype(BF)


def relay(three, arrived):
    return pl.pallas_call(
        relay_body,
        in_specs=[VMEM] * 2,
        out_specs=VMEM,
        out_shape=shape(three.shape, BF),
        compiler_params=params(),
    )(*near_by(three, arrived))


def finish_body(own, one, two, three, stay, give):
    first = lax.axis_index("c") == 0
    height = own.shape[0]
    half = height // 2
    for k in range(2):
        value = one[2 * k].astype(F32) + two[k].astype(F32) + three[k].astype(F32)
        value = value[:height]
        if k == 0:
            value = value + own[...]
        low, high = value[:half], value[half:]
        stay[k] = jnp.where(first, low, high)
        give[k] = jnp.where(first, high, low)


def finish(own, one, two, three):
    height, width = own.shape
    dims = (2, height // 2, width)
    return pl.pallas_call(
        finish_body,
        in_specs=[VMEM] * 4,
        out_specs=[VMEM] * 2,
        out_shape=[shape(dims, F32)] * 2,
        compiler_params=params(),
        cost_estimate=pl.CostEstimate(flops=2 * 10**10, bytes_accessed=4 * 10**7, transcendentals=0),
    )(*near_by(own, one, two, three))


def shards(queries, cotangent, neighbours, present, key_weight, value_weight):
    ny, nz, nx = 4, 8, 4
    core = lax.axis_index("c")
    first = core == 0
    flags = jnp.concatenate([core[None], present.reshape(-1)]).astype(jnp.int32)
    tie = lax.optimization_barrier

    own = neighbours
    opposite, behind, ahead = (hop(own, "x", nx, step) for step in (2, 1, -1))
    flags, start = tie((flags, own))
    key_w, value_w, q, g, own = load(key_weight, value_weight, queries, cotangent, start)
    opposite, own = tie((opposite, own))
    k1, v1 = project((own, opposite), key_w, value_w)
    others = [swap(neighbours), swap(opposite)]
    behind, ahead, k1, v1, *others = tie((behind, ahead, k1, v1, *others))
    k2, v2 = project((behind, ahead), key_w, value_w)
    others += [swap(behind), swap(ahead)]
    k2, *others = tie((k2, *others))
    slabs = (own, opposite, behind, ahead)

    attended, query_grad, keep, send = attend(flags, k1, v1, k2, v2, q, g, own.shape[2])
    received = swap(send)
    partial, turned = weight_grad(slabs, others, keep)
    received, partial = tie((received, partial))
    (far,) = weight_split(turned, received, partial, ny, (1,), (BF,))
    far_in = hop(far, "y", ny, 1)
    far, partial = tie((far, partial))
    mine, back, front = weight_split(
        turned, received, partial, ny, (0, 2, 3), (F32, BF, F32)
    )
    keep, send, front = tie((keep, send, front))
    part, *rest = passage_open(keep, send, key_weight, value_weight)
    back, part = tie((back, part))
    back_in = hop(back, "y", ny, -1)
    p0, p3, p1, p2 = passage_close(keep, send, part, rest, own.shape)
    far_in, p1, p2, p3 = tie((far_in, p1, p2, p3))
    front, front_cross = deal(front, far_in, BF)
    front, front_cross, mine = tie((front, front_cross, mine))
    front_in = hop(front, "y", ny, 1)
    cross_in = hop(front_cross, "y", ny, 1, cross=True)
    base, cross = deal(mine, back_in, F32)
    cross = swap(cross)
    p1_in = hop(p1, "x", nx, -1)
    front_in, cross_in, beyond, p1_in = tie((front_in, cross_in, hop(p3, "x", nx, 1), p1_in))

    here, one, two, three = fold(base, front_in, cross, cross_in, mine.shape[0] // nz)
    one_in = hop(one, "z", nz, 1)
    two_in = hop(two, "z", nz, 2)
    share = add(p2, beyond)
    three, share = tie((relay(three, one_in), share))
    three_in = hop(three, "z", nz, 3)
    returned = [p1_in, hop(share, "x", nx, 1)]
    stay, give = finish(here, one_in, two_in, three_in)
    other = swap(give)
    neighbour_grad = p0
    for r in returned:
        neighbour_grad = neighbour_grad + r.astype(F32)
    main, rest = stay[0] + other[1], stay[1] + other[0]
    return (
        attended,
        query_grad,
        neighbour_grad,
        jnp.where(first, main, rest),
        jnp.where(first, rest, main),
    )


def solution(mesh):
    mesh = Mesh(mesh.devices.reshape(4, 8, 2, 4), ("y", "z", "c", "x"))
    dp = ("y", "z", "c")
    placed = (
        P(dp, "x"),
        P(dp, "x"),
        P(dp, None, "x", None),
        P(dp, None),
        P(None, "x"),
        P(None, "x"),
    )
    return jax.shard_map(
        shards,
        mesh=mesh,
        in_specs=placed,
        out_specs=(
            P(dp, "x"),
            P(dp, "x"),
            P(dp, None, "x", None),
            P(dp, "x"),
            P(dp, "x"),
        ),
        check_vma=False,
    )
```
